256 devices in a mesh: gx: 32 (over z, x_hi, core), gy: 8 (over y, x_lo).
Axes of the slice: x: 4 (x_hi: 2, x_lo: 2; x = x_hi * 2 + x_lo), y: 4, z: 8, core: 2. Of those that a mesh axis runs over, the one named last changes fastest.
Arguments:
- start: float32 [19, 2, 256, 4096], P(None, None, 'gx', 'gy'), may hold values from 0 to 1, as said below
- final_adjoint: float32 [19, 2, 256, 4096], P(None, None, 'gx', 'gy'), may hold values from -6 to 6
- resist: float32 [2, 256, 4096], P(None, 'gx', 'gy'), may hold values from 0.05 to 3
- mask: int32 [2, 256, 4096], P(None, 'gx', 'gy'), may hold values 0 or 1
Outputs:
- adjoint_start: float32 [19, 2, 256, 4096], P(None, None, 'gx', 'gy')
- resist_grad: float32 [2, 256, 4096], P(None, 'gx', 'gy')
The draws below stay inside these ranges and needn't reach their ends.
Inputs may be any that keep to these rules, and one draw needn't show every extreme that they name: `start`: every population is positive, within a factor 0.5 to 1.5 of its lattice weight.
All inputs are finite; a program needn't handle non-finite values. No bound on the sum of `mask` on one device may be relied on, other than what follows from the above.
Results may differ from the reference program's by a relative error of at most 0.0003.
Values sent between devices are 32-bit elements; how exact they have to be, the bound alone decides.
A program may use at most 64 MiB of HBM per device.

```python
import math
import jax
import jax.numpy as jnp
import numpy as np
from jax import lax

Q = 19
NZ = 2
STEPS = 4
CX = 8
NX = 256
NY = 4096


def draw_start(key, part):
    key = jax.random.fold_in(key, 11)
    weights = jnp.asarray(np.array([1.0 / 3.0] + [1.0 / 18.0] * 6 + [1.0 / 36.0] * 12), jnp.float32)
    spread = 1.0 + 0.15 * jax.random.truncated_normal(key, -2.0, 2.0, (Q, NZ, NX, NY), jnp.float32)
    return weights[:, None, None, None] * spread


def place_ends(values, stream_key, low, high):
    place = [jax.random.randint(jax.random.fold_in(stream_key, axis), (), 0, length) for axis, length in enumerate(values.shape)]
    main_axis = values.shape.index(max(values.shape))
    beside = place[:main_axis] + [(place[main_axis] + 1) % values.shape[main_axis]] + place[main_axis + 1:]
    return values.at[tuple(place)].set(low).at[tuple(beside)].set(high)


def levels(rng, extent, pieces, least, top_value):
    factor_of = 1.0
    for dim, blocks in pieces:
        steps = jax.random.uniform(jax.random.fold_in(jax.random.fold_in(rng, 6), dim), (blocks,), jnp.float32, least / len(pieces), top_value / len(pieces))
        factor_of = factor_of * jnp.repeat(jnp.exp(steps), extent[dim] // blocks).reshape((-1,) + (1,) * (len(extent) - 1 - dim))
    return factor_of


def noise(key, shape, deviation, most, shards=(), kind=jnp.bfloat16):
    level = levels(key, shape, shards, -0.22, 0.18) if shards else 1.0
    entries = jax.random.normal(key, shape, jnp.float32) * deviation * level
    return jnp.minimum(jnp.maximum(entries, -most), most).astype(kind)


def setup_inputs(seed: int = 0) -> dict:
    key_of = jax.random.split(jax.random.key(seed), 5)
    return {
        "start": draw_start(jax.random.fold_in(key_of[4], 71), 0),
        "final_adjoint": noise(key_of[1], (Q, NZ, NX, NY), 1.0, 6.0, ((2, 32), (3, 8)), jnp.float32),
        "resist": jnp.clip(jnp.exp(math.log(3.0) - 4.0943445 * jax.random.uniform(key_of[2], (NZ, NX, NY), jnp.float32) ** levels(key_of[2], (NZ, NX, NY), ((1, 32), (2, 8)), -0.2, 0.2)), 0.05, 3.0),
        "mask": place_ends((jax.random.randint(key_of[3], (NZ, NX, NY), 0, 5) < 1).astype(jnp.int32), jax.random.fold_in(key_of[3], 1), 0, 1),
    }


LINKS = np.array([[0, 0, 0], [1, 0, 0], [-1, 0, 0], [0, 1, 0], [0, -1, 0], [0, 0, 1], [0, 0, -1], [1, 1, 0], [-1, -1, 0], [1, -1, 0], [-1, 1, 0], [1, 0, 1], [-1, 0, -1], [1, 0, -1], [-1, 0, 1], [0, 1, 1], [0, -1, -1], [0, 1, -1], [0, -1, 1]], dtype=np.int32)
LINK_WEIGHTS = np.array([1.0 / 3.0] + [1.0 / 18.0] * 6 + [1.0 / 36.0] * 12)
OPPOSITE = [0, 2, 1, 4, 3, 6, 5, 8, 7, 10, 9, 12, 11, 14, 13, 16, 15, 18, 17]
RELAXATION = 1.25

def collide(pops, resist, solid):
    shape = (19,) + (1,) * (pops.ndim - 1)
    step_x = jnp.asarray(LINKS[:, 0], pops.dtype).reshape(shape)
    step_y = jnp.asarray(LINKS[:, 1], pops.dtype).reshape(shape)
    step_z = jnp.asarray(LINKS[:, 2], pops.dtype).reshape(shape)
    weights = jnp.asarray(LINK_WEIGHTS, pops.dtype).reshape(shape)
    density = lax.optimization_barrier(jnp.sum(pops, axis=0))
    factor = 1.0 / (density * (1.0 + resist))
    vel_x = lax.optimization_barrier(jnp.sum(step_x * pops, axis=0)) * factor
    vel_y = lax.optimization_barrier(jnp.sum(step_y * pops, axis=0)) * factor
    vel_z = lax.optimization_barrier(jnp.sum(step_z * pops, axis=0)) * factor
    speed = vel_x * vel_x + vel_y * vel_y + vel_z * vel_z
    along = step_x * vel_x + step_y * vel_y + step_z * vel_z
    equil = weights * density * (1.0 + 3.0 * along + 4.5 * along * along - 1.5 * speed)
    relaxed = pops - RELAXATION * (pops - equil)
    bounced = jnp.stack([pops[member] for member in OPPOSITE])
    return relaxed + solid * (bounced - relaxed)

def split_q(array):
    return jnp.moveaxis(array.reshape(array.shape[0], NZ, NX // CX, CX, NY), 2, 0)

def split_z(array):
    return jnp.moveaxis(array.reshape(NZ, NX // CX, CX, NY), 1, 0)

def join_q(array):
    return jnp.moveaxis(array, 0, 2).reshape(array.shape[1], NZ, NX, NY)

def join_z(array):
    return jnp.moveaxis(array, 0, 1).reshape(NZ, NX, NY)

def stream(post, sign):
    moved = []
    for member in range(19):
        shifts = (sign * int(LINKS[member, 2]), sign * int(LINKS[member, 0]), sign * int(LINKS[member, 1]))
        moved.append(jnp.roll(post[member], shifts, axis=(0, 1, 2)))
    return jnp.stack(moved)

def advance(pops, resist, solid):

    def single(items):
        return collide(items[0], items[1], items[2])
    post = join_q(lax.map(single, (split_q(pops), split_z(resist), split_z(solid))))
    return stream(post, 1)

def pullback(pops, resist, solid, cotangent):

    def single(items):
        block_solid = items[2]
        _, puller = jax.vjp(lambda first, second: collide(first, second, block_solid), items[0], items[1])
        return puller(items[3])
    back_pops, back_resist = lax.map(single, (split_q(pops), split_z(resist), split_z(solid), split_q(cotangent)))
    return (join_q(back_pops), join_z(back_resist))

def reference(start, final_adjoint, resist, mask):
    solid = mask.astype(start.dtype)
    adjoint = final_adjoint
    gradient = jnp.zeros(resist.shape, start.dtype)
    for section in reversed(range(STEPS)):
        state = start
        for before in range(section):
            state = advance(state, resist, solid)
        incoming = stream(adjoint, -1)
        adjoint, contrib = pullback(state, resist, solid, incoming)
        gradient = gradient + contrib
    return (adjoint, gradient)
```

```python
import functools

import jax
import jax.numpy as jnp
from jax import lax
from jax.experimental import pallas as pl
from jax.experimental.pallas import tpu as pltpu
from jax.sharding import PartitionSpec as P

MESH = pl.DeviceIdType.MESH
F32 = jnp.float32
OMEGA = 1.25
KEEP = 1.0 - OMEGA

LINKS = [
    (0, 0, 0),
    (1, 0, 0), (-1, 0, 0), (0, 1, 0), (0, -1, 0), (0, 0, 1), (0, 0, -1),
    (1, 1, 0), (-1, -1, 0), (1, -1, 0), (-1, 1, 0),
    (1, 0, 1), (-1, 0, -1), (1, 0, -1), (-1, 0, 1),
    (0, 1, 1), (0, -1, -1), (0, 1, -1), (0, -1, 1),
]
Q = 19
UP = [1, 7, 9, 11, 13]
FLAT = [0, 3, 4, 5, 6, 15, 16, 17, 18]
DOWN = [2, 8, 10, 12, 14]
DRAG, SOLID, ITEMS = 14, 15, 21
POST = {q: k for k, q in enumerate(UP + FLAT)} | {q: 16 + k for k, q in enumerate(DOWN)}
ADJ = {q: k for k, q in enumerate(UP + FLAT + DOWN)}

ROWS = 8
COLS = 6
SLOTS = 10
PACK = 4


def mask_lanes(low, high, period):
    lane = lax.broadcasted_iota(jnp.int32, (8, 128), 1) % period
    return (lane >= low) & (lane < high)


def row_at(ref, item, row):
    return ref[item, pl.ds(pl.multiple_of((row + 8) * 8, 8), 8), :]


def set_row(ref, item, row, value):
    ref[item, pl.ds(pl.multiple_of((row + 8) * 8, 8), 8), :] = value


def shift_row(value, dy, dz):
    if dz:
        value = pltpu.roll(value, 4, 0)
    if dy:
        lane = lax.broadcasted_iota(jnp.int32, (8, 128), 1)
        moved = pltpu.roll(value, dy % 128, 1)
        beside = pltpu.roll(moved, dy % 8, 0)
        value = jnp.where(lane == (0 if dy > 0 else 127), beside, moved)
    return value


def shift_strip(value, dx, dy, dz):
    if dx:
        value = pltpu.roll(value, dx % 24, 0)
    turn = (dy + 64 * abs(dz)) % 128
    if turn:
        value = pltpu.roll(value, turn, 1)
    return value


def moments(f, drag):
    total = {}
    diff = {}
    for q in range(1, Q, 2):
        total[q] = f[q] + f[q + 1]
        diff[q] = f[q] - f[q + 1]
    rho = f[0] + ((total[1] + total[3]) + (total[5] + total[7])) + (
        (total[9] + total[11]) + (total[13] + (total[15] + total[17]))
    )
    scale = drag / rho
    ux = ((diff[1] + diff[7]) + (diff[9] + diff[11]) + diff[13]) * scale
    uy = ((diff[3] + diff[7]) + (diff[15] - diff[9]) + diff[17]) * scale
    uz = ((diff[5] + diff[11]) + (diff[15] - diff[13]) - diff[17]) * scale
    return rho, ux, uy, uz


def along(vec, q):
    out = None
    for part, c in zip(vec, LINKS[q]):
        if c:
            if out is None:
                out = part
            else:
                out = out + part if c > 0 else out - part
    return out


def relax(f, rho, u, solid):
    w2 = rho * (OMEGA / 36.0)
    b = [x * (w2 * 3.0) for x in u]
    h = [x * 1.5 for x in u]
    base = w2 - (u[0] * b[0] + u[1] * b[1] + u[2] * b[2]) * 0.5
    blocked = solid > 0.5
    post = {}
    post[0] = jnp.where(blocked, f[0], KEEP * f[0] + 12.0 * base)
    twice = base + base
    for q in range(1, Q, 2):
        cb, ch = along(b, q), along(h, q)
        if q < 7:
            cb = cb + cb
            even = twice + cb * ch
        else:
            even = base + cb * ch
        post[q] = jnp.where(blocked, f[q + 1], KEEP * f[q] + (even + cb))
        post[q + 1] = jnp.where(blocked, f[q], KEEP * f[q + 1] + (even - cb))
    return post


def pull(inc, rho, u, drag, solid):
    ux, uy, uz = u
    blocked = solid > 0.5
    s, d = {}, {}
    for q in range(1, Q, 2):
        s[q] = inc[q] + inc[q + 1]
        d[q] = inc[q] - inc[q + 1]
    sxy, sxz, syz = s[7] + s[9], s[11] + s[13], s[15] + s[17]
    kxx = (s[1] + s[1]) + sxy + sxz
    kyy = (s[3] + s[3]) + sxy + syz
    kzz = (s[5] + s[5]) + sxz + syz
    kxy, kxz, kyz = s[7] - s[9], s[11] - s[13], s[15] - s[17]
    k0 = 12.0 * inc[0] + 2.0 * (s[1] + s[3] + s[5]) + (sxy + sxz + syz)
    kx = (d[1] + d[1]) + (d[7] + d[9]) + (d[11] + d[13])
    ky = (d[3] + d[3]) + (d[7] - d[9]) + (d[15] + d[17])
    kz = (d[5] + d[5]) + (d[11] - d[13]) + (d[15] - d[17])
    wk = OMEGA / 36.0
    vx = kxx * ux + kxy * uy + kxz * uz
    vy = kxy * ux + kyy * uy + kyz * uz
    vz = kxz * ux + kyz * uy + kzz * uz
    gx = 3.0 * (kx - k0 * ux) + 9.0 * vx
    gy = 3.0 * (ky - k0 * uy) + 9.0 * vy
    gz = 3.0 * (kz - k0 * uz) + 9.0 * vz
    uu = ux * ux + uy * uy + uz * uz
    uku = ux * vx + uy * vy + uz * vz
    grho = wk * (k0 + 1.5 * (k0 * uu) - 4.5 * uku)
    ku = kx * ux + ky * uy + kz * uz
    du = 3.0 * (ku - k0 * uu) + 9.0 * uku
    scale = wk * drag
    g = (gx * scale, gy * scale, gz * scale)
    back = jnp.where(blocked, 0.0, (rho * du) * (-scale))
    out = {0: jnp.where(blocked, inc[0], KEEP * inc[0] + grho)}
    for q in range(1, Q, 2):
        cg = along(g, q)
        out[q] = jnp.where(blocked, inc[q + 1], KEEP * inc[q] + (grho + cg))
        out[q + 1] = jnp.where(blocked, inc[q], KEEP * inc[q + 1] + (grho - cg))
    return out, back


def kernel(
    n_gx, n_gy, start_hbm, adj_hbm, resist_hbm, mask_hbm, out_ref, grad_ref,
    start, adj, resist, mask, p0, p1, p2, q0, q1, q2, q3, m0, m1, m2, m3, sums,
    s0, s1, s2, t0, t1, t2, t3, k0, k1, k2, k3, back_strip, packs, got,
    load_sem, send_sem, recv_sem,
):
    gx, gy = lax.axis_index("gx"), lax.axis_index("gy")

    def device(dx, dy):
        return (lax.rem(gx + dx + n_gx, n_gx), lax.rem(gy + dy + n_gy, n_gy))

    around = [(dx, dy) for dx in (-1, 0, 1) for dy in (-1, 0, 1) if dx or dy]
    barrier = pltpu.get_barrier_semaphore()
    for dx, dy in around:
        pl.semaphore_signal(barrier, inc=1, device_id=device(dx, dy), device_id_type=MESH)

    loads = [
        pltpu.make_async_copy(src, dst, load_sem.at[k])
        for k, (src, dst) in enumerate(
            ((start_hbm, start), (resist_hbm, resist), (mask_hbm, mask), (adj_hbm, adj))
        )
    ]
    for copy in loads:
        copy.start()
    for copy in loads[:3]:
        copy.wait()

    def first(k, _):
        here = pl.ds(pl.multiple_of(k * 8, 8), 8)
        there = pl.ds(64 + k, 8, stride=8)
        f = {q: start[q, here, :] for q in range(Q)}
        drag = 1.0 / (1.0 + resist[here, :])
        solid = mask[here, :].astype(F32)
        rho, *u = moments(f, drag)
        post = relax(f, rho, u, solid)
        for q in range(Q):
            p0[POST[q], there, :] = post[q]
        p0[DRAG, there, :] = drag
        p0[SOLID, there, :] = solid
        for item, value in enumerate((rho, *u)):
            m0[item, there, :] = value
        return 0

    lax.fori_loop(0, 8, first, 0, unroll=4)
    loads[3].wait()

    def turn(k, _):
        here = pl.ds(pl.multiple_of(k * 8, 8), 8)
        there = pl.ds(64 + k, 8, stride=8)
        for q in range(Q):
            q0[ADJ[q], there, :] = adj[q, here, :]
        return 0

    lax.fori_loop(0, 8, turn, 0)

    low0, low1, low2 = mask_lanes(0, 32, 128), mask_lanes(64, 96, 128), mask_lanes(32, 64, 128)

    def own_strip(src, item, tile):
        def part(k, by):
            return pltpu.roll(src[item, pl.ds(tile * 64 + k, 8, stride=8), :], by, 1)

        return jnp.where(
            low0, part(0, 6), jnp.where(low1, part(4, 70), jnp.where(low2, part(3, 44), part(7, 108)))
        )

    sides = [[None] * PACK, [None] * PACK]
    for item in range(ITEMS + Q):
        slot, place = item % SLOTS, item // SLOTS
        src, dst, index = (p0, s0, item) if item < ITEMS else (q0, t0, item - ITEMS)
        strip = own_strip(src, index, 1)
        dst[index, 8:16, :] = strip
        chosen = mask_lanes(slot * COLS, slot * COLS + COLS, 64)
        for side, lane in ((0, 6), (1, 38)):
            moved = pltpu.roll(strip, (slot * COLS - lane) % 128, 1)
            old = sides[side][place]
            sides[side][place] = moved if old is None else jnp.where(chosen, moved, old)
    for side in range(2):
        for place in range(PACK):
            packs[side, place] = sides[side][place]

    pl.semaphore_wait(barrier, len(around))

    copies = []

    def send(src, dst, dx, dy):
        k = len(copies)
        copy = pltpu.make_async_remote_copy(
            src_ref=src, dst_ref=dst, send_sem=send_sem.at[k], recv_sem=recv_sem.at[k],
            device_id=device(dx, dy), device_id_type=MESH,
        )
        copy.start()
        copies.append(copy)

    def span(ref, low, high, row, count):
        return ref.at[pl.ds(low, high - low), pl.ds((row + 8) * 8, count * 8), :]

    def both(ref, low, high, row, count, dx):
        send(span(ref, low, high, row, count), span(ref, low, high, row - 8 * dx, count), dx, 0)

    for dx, dy in around:
        if dy:
            send(packs.at[(dy + 1) // 2], got.at[1 - dx, (1 - dy) // 2], dx, dy)
    both(p0, 0, 21, 4, 4, 1)
    both(p0, 0, 21, 0, 4, -1)
    both(p0, 0, 16, 3, 1, 1)
    both(p0, 5, 21, 4, 1, -1)
    both(p0, 0, 5, 2, 1, 1)
    both(p0, 16, 21, 5, 1, -1)
    posts = len(copies)
    both(q0, 0, 19, 6, 2, 1)
    both(q0, 0, 19, 0, 2, -1)
    both(q0, 5, 19, 5, 1, 1)
    both(q0, 0, 14, 2, 1, -1)
    both(q0, 14, 19, 4, 1, 1)
    both(q0, 0, 5, 3, 1, -1)

    def forward(src, dst, mom, row):
        f = {
            q: shift_row(row_at(src, POST[q], row - LINKS[q][0]), LINKS[q][1], LINKS[q][2])
            for q in range(Q)
        }
        rho, *u = moments(f, row_at(p0, DRAG, row))
        for item, value in enumerate((rho, *u)):
            set_row(mom, item, row, value)
        if dst is not None:
            post = relax(f, rho, u, row_at(p0, SOLID, row))
            for q in range(Q):
                set_row(dst, POST[q], row, post[q])

    def backward(src, dst, mom, row):
        inc = {
            q: shift_row(row_at(src, ADJ[q], row + LINKS[q][0]), -LINKS[q][1], LINKS[q][2])
            for q in range(Q)
        }
        rho, *u = [row_at(mom, item, row) for item in range(4)]
        return pull(inc, rho, u, row_at(p0, DRAG, row), row_at(p0, SOLID, row))

    def middle(src, dst, mom, row):
        out, back = backward(src, dst, mom, row)
        for q in range(Q):
            set_row(dst, ADJ[q], row, out[q])
        place = pl.ds(pl.multiple_of((row + 8) * 8, 8), 8)
        sums[place, :] = back if mom is m3 else sums[place, :] + back

    def rows(body, low, high, *refs):
        def one(row, _):
            body(*refs, row)
            return 0

        lax.fori_loop(low, high, one, 0, unroll=4)

    def rim(body, low, high, *refs):
        n = high - low

        def one(k, _):
            body(*refs, jnp.where(k < n, k + low, 7 - low + n - k))
            return 0

        lax.fori_loop(0, 2 * n, one, 0, unroll=4)

    rows(forward, 1, 7, p0, p1, m1)
    rows(forward, 2, 6, p1, p2, m2)
    rows(forward, 3, 5, p2, None, m3)

    for copy in copies[:posts]:
        copy.wait_recv()
    rim(forward, -5, 1, p0, p1, m1)
    rim(forward, -4, 2, p1, p2, m2)
    rim(forward, -3, 3, p2, None, m3)

    left, right = mask_lanes(0, COLS, 64), mask_lanes(44, 44 + COLS, 64)

    def halo_strip(strip, tile, item, slot, place):
        by = slot * COLS
        low = pltpu.roll(got[tile, 0, place], (-by) % 128, 1)
        high = pltpu.roll(got[tile, 1, place], (44 - by) % 128, 1)
        return jnp.where(left, low, jnp.where(right, high, strip))

    def fill_strips(src, dst, first_item, count):
        for item in range(count):
            slot, place = (first_item + item) % SLOTS, (first_item + item) // SLOTS
            for tile in range(3):
                strip = dst[item, 8:16, :] if tile == 1 else own_strip(src, item, tile)
                dst[item, 8 * tile : 8 * tile + 8, :] = halo_strip(strip, tile, item, slot, place)

    fill_strips(p0, s0, 0, ITEMS)

    def strip_forward(src, dst, mom):
        f = {q: shift_strip(src[POST[q]], *LINKS[q]) for q in range(Q)}
        rho, *u = moments(f, s0[DRAG])
        for item, value in enumerate((rho, *u)):
            mom[item] = value
        if dst is not None:
            post = relax(f, rho, u, s0[SOLID])
            for q in range(Q):
                dst[POST[q]] = post[q]

    for item in range(4):
        k0[item, 8:16, :] = own_strip(m0, item, 1)
    strip_forward(s0, s1, k1)
    strip_forward(s1, s2, k2)
    strip_forward(s2, None, k3)

    def strip_backward(src, mom):
        inc = {q: shift_strip(src[ADJ[q]], *[-c for c in LINKS[q]]) for q in range(Q)}
        rho, *u = [mom[item] for item in range(4)]
        return pull(inc, rho, u, s0[DRAG], s0[SOLID])

    def strip_middle(src, dst, mom):
        out, back = strip_backward(src, mom)
        for q in range(Q):
            dst[ADJ[q]] = out[q]
        back_strip[...] = back if mom is k3 else back_strip[...] + back

    rows(middle, 1, 7, q0, q1, m3)
    rows(middle, 2, 6, q1, q2, m2)
    rows(middle, 3, 5, q2, q3, m1)

    for copy in copies[posts:]:
        copy.wait_recv()
    fill_strips(q0, t0, ITEMS, Q)
    strip_middle(t0, t1, k3)
    strip_middle(t1, t2, k2)
    strip_middle(t2, t3, k1)
    strip_out, strip_back = strip_backward(t3, k0)
    for q in range(Q):
        t1[ADJ[q], 8:16, :] = strip_out[q][8:16]
    back_strip[8:16, :] = back_strip[8:16, :] + strip_back[8:16]

    rim(middle, -3, 1, q0, q1, m3)
    rim(middle, -2, 2, q1, q2, m2)
    rim(middle, -1, 3, q2, q3, m1)

    def final(row, _):
        out, back = backward(q3, None, m0, row)
        there = pl.ds(row, 8, stride=8)
        for q in range(Q):
            out_ref[q, there, :] = out[q]
        grad_ref[there, :] = row_at_sum(row) + back
        return 0

    def row_at_sum(row):
        return sums[pl.ds(pl.multiple_of((row + 8) * 8, 8), 8), :]

    lax.fori_loop(0, 8, final, 0, unroll=4)

    edge_low, edge_high = mask_lanes(0, COLS, 128), mask_lanes(128 - COLS, 128, 128)

    def merge(ref, strip):
        for k, lane, chosen in ((0, 6, edge_low), (4, 70, edge_low), (3, 38 - 122, edge_high), (7, 102 - 122, edge_high)):
            here = slice(8 * k, 8 * k + 8)
            ref[here, :] = jnp.where(chosen, pltpu.roll(strip, (-lane) % 128, 1), ref[here, :])

    for q in range(Q):
        merge(out_ref.at[q], t1[ADJ[q], 8:16, :])
    merge(grad_ref, back_strip[8:16, :])

    for copy in copies:
        copy.wait_send()


def to_tiles(a):
    lead = a.shape[:-3]
    n = len(lead)
    a = a.reshape(*lead, 2, 8, 4, 128)
    a = a.transpose(*range(n), n, n + 2, n + 1, n + 3)
    return a.reshape(*lead, 64, 128)


def from_tiles(a):
    lead = a.shape[:-2]
    n = len(lead)
    a = a.reshape(*lead, 2, 4, 8, 128)
    a = a.transpose(*range(n), n, n + 2, n + 1, n + 3)
    return a.reshape(*lead, 2, 8, 512)


def solution(mesh):
    n_gx, n_gy = mesh.shape["gx"], mesh.shape["gy"]

    def local(start, final_adjoint, resist, mask):
        any_space = pl.BlockSpec(memory_space=pl.ANY)
        vmem = pl.BlockSpec(memory_space=pltpu.VMEM)
        buf = lambda *shape: pltpu.VMEM(shape, F32)
        out, grad = pl.pallas_call(
            functools.partial(kernel, n_gx, n_gy),
            out_shape=(
                jax.ShapeDtypeStruct((Q, 64, 128), F32),
                jax.ShapeDtypeStruct((64, 128), F32),
            ),
            in_specs=[any_space] * 4,
            out_specs=[vmem, vmem],
            scratch_shapes=[
                buf(Q, 64, 128), buf(Q, 64, 128), buf(64, 128), pltpu.VMEM((64, 128), jnp.int32),
                buf(ITEMS, 192, 128), buf(ITEMS, 192, 128), buf(ITEMS, 192, 128),
                buf(Q, 192, 128), buf(Q, 192, 128), buf(Q, 192, 128), buf(Q, 192, 128),
                buf(4, 192, 128), buf(4, 192, 128), buf(4, 192, 128), buf(4, 192, 128), buf(192, 128),
                buf(ITEMS, 24, 128), buf(ITEMS, 24, 128), buf(ITEMS, 24, 128),
                buf(Q, 24, 128), buf(Q, 24, 128), buf(Q, 24, 128), buf(Q, 24, 128),
                buf(4, 24, 128), buf(4, 24, 128), buf(4, 24, 128), buf(4, 24, 128), buf(24, 128),
                buf(2, PACK, 8, 128), buf(3, 2, PACK, 8, 128),
                pltpu.SemaphoreType.DMA((4,)),
                pltpu.SemaphoreType.DMA((18,)),
                pltpu.SemaphoreType.DMA((18,)),
            ],
            compiler_params=pltpu.CompilerParams(
                collective_id=0, has_side_effects=True, vmem_limit_bytes=63 * 2**20
            ),
        )(to_tiles(start), to_tiles(final_adjoint), to_tiles(resist), to_tiles(mask))
        return from_tiles(out), from_tiles(grad)

    return jax.shard_map(
        local,
        mesh=mesh,
        in_specs=(
            P(None, None, "gx", "gy"),
            P(None, None, "gx", "gy"),
            P(None, "gx", "gy"),
            P(None, "gx", "gy"),
        ),
        out_specs=(P(None, None, "gx", "gy"), P(None, "gx", "gy")),
        check_vma=False,
    )
```

```python
import functools

import jax
import jax.numpy as jnp
from jax import lax
from jax.experimental import pallas as pl
from jax.experimental.pallas import tpu as pltpu
from jax.sharding import PartitionSpec as P

MESH = pl.DeviceIdType.MESH
F32 = jnp.float32
OMEGA = 1.25
KEEP = 1.0 - OMEGA

LINKS = [
    (0, 0, 0),
    (1, 0, 0), (-1, 0, 0), (0, 1, 0), (0, -1, 0), (0, 0, 1), (0, 0, -1),
    (1, 1, 0), (-1, -1, 0), (1, -1, 0), (-1, 1, 0),
    (1, 0, 1), (-1, 0, -1), (1, 0, -1), (-1, 0, 1),
    (0, 1, 1), (0, -1, -1), (0, 1, -1), (0, -1, 1),
]
Q = 19
UP = [1, 7, 9, 11, 13]
FLAT = [0, 3, 4, 5, 6, 15, 16, 17, 18]
DOWN = [2, 8, 10, 12, 14]
DRAG, SOLID, ITEMS = 19, 20, 21
ADJ = POST = {q: k for k, q in enumerate(UP + FLAT + DOWN)}

ROWS = 8
COLS = 6
SLOTS = 10
PACK = 4


def mask_lanes(low, high, period):
    lane = lax.broadcasted_iota(jnp.int32, (8, 128), 1) % period
    return (lane >= low) & (lane < high)


def row_at(ref, item, row):
    return ref[item, pl.ds(pl.multiple_of((row + 8) * 8, 8), 8), :]


def set_row(ref, item, row, value):
    ref[item, pl.ds(pl.multiple_of((row + 8) * 8, 8), 8), :] = value


def shift_row(value, dy, dz):
    if dz:
        value = pltpu.roll(value, 4, 0)
    if dy:
        lane = lax.broadcasted_iota(jnp.int32, (8, 128), 1)
        moved = pltpu.roll(value, dy % 128, 1)
        beside = pltpu.roll(moved, dy % 8, 0)
        value = jnp.where(lane == (0 if dy > 0 else 127), beside, moved)
    return value


def shift_strip(value, dx, dy, dz):
    if dx:
        value = pltpu.roll(value, dx % 24, 0)
    turn = (dy + 64 * abs(dz)) % 128
    if turn:
        value = pltpu.roll(value, turn, 1)
    return value


def moments(f, drag):
    total = {}
    diff = {}
    for q in range(1, Q, 2):
        total[q] = f[q] + f[q + 1]
        diff[q] = f[q] - f[q + 1]
    rho = f[0] + ((total[1] + total[3]) + (total[5] + total[7])) + (
        (total[9] + total[11]) + (total[13] + (total[15] + total[17]))
    )
    scale = drag / rho
    ux = ((diff[1] + diff[7]) + (diff[9] + diff[11]) + diff[13]) * scale
    uy = ((diff[3] + diff[7]) + (diff[15] - diff[9]) + diff[17]) * scale
    uz = ((diff[5] + diff[11]) + (diff[15] - diff[13]) - diff[17]) * scale
    return rho, ux, uy, uz


def along(vec, q):
    out = None
    for part, c in zip(vec, LINKS[q]):
        if c:
            if out is None:
                out = part
            else:
                out = out + part if c > 0 else out - part
    return out


def relax(f, rho, u, solid):
    w2 = rho * (OMEGA / 36.0)
    b = [x * (w2 * 3.0) for x in u]
    h = [x * 1.5 for x in u]
    base = w2 - (u[0] * b[0] + u[1] * b[1] + u[2] * b[2]) * 0.5
    blocked = solid > 0.5
    post = {}
    post[0] = jnp.where(blocked, f[0], KEEP * f[0] + 12.0 * base)
    twice = base + base
    for q in range(1, Q, 2):
        cb, ch = along(b, q), along(h, q)
        if q < 7:
            cb = cb + cb
            even = twice + cb * ch
        else:
            even = base + cb * ch
        post[q] = jnp.where(blocked, f[q + 1], KEEP * f[q] + (even + cb))
        post[q + 1] = jnp.where(blocked, f[q], KEEP * f[q + 1] + (even - cb))
    return post


def pull(inc, rho, u, drag, solid):
    ux, uy, uz = u
    blocked = solid > 0.5
    s, d = {}, {}
    for q in range(1, Q, 2):
        s[q] = inc[q] + inc[q + 1]
        d[q] = inc[q] - inc[q + 1]
    sxy, sxz, syz = s[7] + s[9], s[11] + s[13], s[15] + s[17]
    kxx = (s[1] + s[1]) + sxy + sxz
    kyy = (s[3] + s[3]) + sxy + syz
    kzz = (s[5] + s[5]) + sxz + syz
    kxy, kxz, kyz = s[7] - s[9], s[11] - s[13], s[15] - s[17]
    k0 = 12.0 * inc[0] + 2.0 * (s[1] + s[3] + s[5]) + (sxy + sxz + syz)
    kx = (d[1] + d[1]) + (d[7] + d[9]) + (d[11] + d[13])
    ky = (d[3] + d[3]) + (d[7] - d[9]) + (d[15] + d[17])
    kz = (d[5] + d[5]) + (d[11] - d[13]) + (d[15] - d[17])
    wk = OMEGA / 36.0
    vx = kxx * ux + kxy * uy + kxz * uz
    vy = kxy * ux + kyy * uy + kyz * uz
    vz = kxz * ux + kyz * uy + kzz * uz
    gx = 3.0 * (kx - k0 * ux) + 9.0 * vx
    gy = 3.0 * (ky - k0 * uy) + 9.0 * vy
    gz = 3.0 * (kz - k0 * uz) + 9.0 * vz
    uu = ux * ux + uy * uy + uz * uz
    uku = ux * vx + uy * vy + uz * vz
    grho = wk * (k0 + 1.5 * (k0 * uu) - 4.5 * uku)
    ku = kx * ux + ky * uy + kz * uz
    du = 3.0 * (ku - k0 * uu) + 9.0 * uku
    scale = wk * drag
    g = (gx * scale, gy * scale, gz * scale)
    back = jnp.where(blocked, 0.0, (rho * du) * (-scale))
    out = {0: jnp.where(blocked, inc[0], KEEP * inc[0] + grho)}
    for q in range(1, Q, 2):
        cg = along(g, q)
        out[q] = jnp.where(blocked, inc[q + 1], KEEP * inc[q] + (grho + cg))
        out[q + 1] = jnp.where(blocked, inc[q], KEEP * inc[q + 1] + (grho - cg))
    return out, back


def kernel(
    n_gx, n_gy, start_hbm, adj_hbm, resist_hbm, mask_hbm, out_ref, grad_ref,
    start, adj, resist, mask, p0, p1, p2, q0, q1, q2, q3, m0, m1, m2, m3, sums,
    s0, s1, s2, t0, t1, t2, t3, k0, k1, k2, k3, back_strip, packs, got, edges, got_edges,
    load_sem, send_sem, recv_sem,
):
    gx, gy = lax.axis_index("gx"), lax.axis_index("gy")

    def device(dx, dy):
        return (lax.rem(gx + dx + n_gx, n_gx), lax.rem(gy + dy + n_gy, n_gy))

    around = [(dx, dy) for dx in (-1, 0, 1) for dy in (-1, 0, 1) if dx or dy]
    barrier = pltpu.get_barrier_semaphore()
    for dx, dy in around:
        pl.semaphore_signal(barrier, inc=1, device_id=device(dx, dy), device_id_type=MESH)

    loads = [
        pltpu.make_async_copy(src, dst, load_sem.at[k])
        for k, (src, dst) in enumerate(
            ((start_hbm, start), (resist_hbm, resist), (mask_hbm, mask), (adj_hbm, adj))
        )
    ]
    for copy in loads:
        copy.start()
    for copy in loads[:3]:
        copy.wait()

    def first(k, _):
        here = pl.ds(pl.multiple_of(k * 8, 8), 8)
        there = pl.ds(64 + k, 8, stride=8)
        f = {q: start[q, here, :] for q in range(Q)}
        drag = 1.0 / (1.0 + resist[here, :])
        solid = mask[here, :].astype(F32)
        rho, *u = moments(f, drag)
        post = relax(f, rho, u, solid)
        for q in range(Q):
            p0[POST[q], there, :] = post[q]
        p0[DRAG, there, :] = drag
        p0[SOLID, there, :] = solid
        for item, value in enumerate((rho, *u)):
            m0[item, there, :] = value
        return 0

    lax.fori_loop(0, 8, first, 0, unroll=4)
    pl.semaphore_wait(barrier, len(around))

    copies = []
    whole = [(gx != n_gx - 1, gx != 0), (gx == n_gx - 1, gx == 0)]

    def send(src, dst, dx, dy, which=None):
        k = len(copies)
        copy = pltpu.make_async_remote_copy(
            src_ref=src, dst_ref=dst, send_sem=send_sem.at[k], recv_sem=recv_sem.at[k],
            device_id=device(dx, dy), device_id_type=MESH,
        )
        if which is None:
            copy.start()
        else:
            pl.when(whole[which][0])(copy.start)
        copies.append((copy, which))
        return copy, which

    def received(*batches):
        for copy, which in batches:
            if which is None:
                copy.wait_recv()
            else:
                pl.when(whole[which][1])(copy.wait_recv)

    def sent(*batches):
        for copy, which in batches:
            if which is None:
                copy.wait_send()
            else:
                pl.when(whole[which][0])(copy.wait_send)

    def span(ref, low, high, row, count):
        return ref.at[pl.ds(low, high - low), pl.ds((row + 8) * 8, count * 8), :]

    def both(ref, low, high, row, count, dx, which=None):
        there = span(ref, low, high, row - 8 * dx, count)
        return send(span(ref, low, high, row, count), there, dx, 0, which)

    posts = (
        both(p0, 0, 19, 7, 1, 1), both(p0, 0, 19, 0, 1, -1),
        both(p0, 19, 21, 5, 3, 1), both(p0, 19, 21, 0, 3, -1),
        both(p0, 0, 14, 6, 1, 1), both(p0, 5, 19, 1, 1, -1),
        both(p0, 0, 5, 5, 1, 1), both(p0, 14, 19, 2, 1, -1),
    )

    loads[3].wait()

    def turn(k, _):
        here = pl.ds(pl.multiple_of(k * 8, 8), 8)
        there = pl.ds(64 + k, 8, stride=8)
        for q in range(Q):
            q0[ADJ[q], there, :] = adj[q, here, :]
        return 0

    lax.fori_loop(0, 8, turn, 0)

    low0, low1, low2 = mask_lanes(0, 32, 128), mask_lanes(64, 96, 128), mask_lanes(32, 64, 128)

    def own_strip(src, item, tile):
        def part(k, by):
            return pltpu.roll(src[item, pl.ds(tile * 64 + k, 8, stride=8), :], by, 1)

        return jnp.where(
            low0, part(0, 6), jnp.where(low1, part(4, 70), jnp.where(low2, part(3, 44), part(7, 108)))
        )

    sides = [[None] * PACK, [None] * PACK]
    for item in range(ITEMS + Q):
        slot, place = item % SLOTS, item // SLOTS
        src, dst, index = (p0, s0, item) if item < ITEMS else (q0, t0, item - ITEMS)
        strip = own_strip(src, index, 1)
        dst[index, 8:16, :] = strip
        chosen = mask_lanes(slot * COLS, slot * COLS + COLS, 64)
        for side, lane in ((0, 6), (1, 38)):
            moved = pltpu.roll(strip, (slot * COLS - lane) % 128, 1)
            old = sides[side][place]
            sides[side][place] = moved if old is None else jnp.where(chosen, moved, old)
    for side in range(2):
        for place in range(PACK):
            packs[side, place] = sides[side][place]

    deeper = (
        both(p0, 14, 19, 6, 1, 1, 1), both(p0, 5, 19, 5, 1, 1, 1), both(p0, 19, 21, 3, 2, 1, 1),
        both(p0, 0, 19, 4, 1, 1, 1), both(p0, 0, 14, 3, 1, 1, 1), both(p0, 0, 5, 2, 1, 1, 1),
    )

    strips = [
        send(packs.at[(dy + 1) // 2], got.at[1 - dx, (1 - dy) // 2], dx, dy)
        for dx, dy in around
        if dy
    ]

    def forward(src, dst, mom, row):
        f = {
            q: shift_row(row_at(src, POST[q], row - LINKS[q][0]), LINKS[q][1], LINKS[q][2])
            for q in range(Q)
        }
        rho, *u = moments(f, row_at(p0, DRAG, row))
        for item, value in enumerate((rho, *u)):
            set_row(mom, item, row, value)
        if dst is not None:
            post = relax(f, rho, u, row_at(p0, SOLID, row))
            for q in range(Q):
                set_row(dst, POST[q], row, post[q])

    def backward(src, dst, mom, row):
        inc = {
            q: shift_row(row_at(src, ADJ[q], row + LINKS[q][0]), -LINKS[q][1], LINKS[q][2])
            for q in range(Q)
        }
        rho, *u = [row_at(mom, item, row) for item in range(4)]
        return pull(inc, rho, u, row_at(p0, DRAG, row), row_at(p0, SOLID, row))

    def middle(src, dst, mom, row):
        out, back = backward(src, dst, mom, row)
        for q in range(Q):
            set_row(dst, ADJ[q], row, out[q])
        place = pl.ds(pl.multiple_of((row + 8) * 8, 8), 8)
        sums[place, :] = back if mom is m3 else sums[place, :] + back

    def rows(body, low, high, *refs):
        def one(row, _):
            body(*refs, row)
            return 0

        lax.fori_loop(low, high, one, 0, unroll=min(3, high - low))

    def rim(body, low, high, *refs):
        n = high - low

        def one(k, _):
            body(*refs, jnp.where(k < n, k + low, 7 - low + n - k))
            return 0

        lax.fori_loop(0, 2 * n, one, 0, unroll=min(3, 2 * n))

    rows(forward, 1, 7, p0, p1, m1)
    rows(forward, 2, 6, p1, p2, m2)
    rows(forward, 3, 5, p2, None, m3)

    adjoints = (
        both(q0, 0, 19, 6, 2, 1), both(q0, 0, 19, 0, 2, -1),
        both(q0, 5, 19, 5, 1, 1), both(q0, 0, 14, 2, 1, -1),
        both(q0, 14, 19, 4, 1, 1), both(q0, 0, 5, 3, 1, -1),
    )

    received(*posts)
    rim(forward, -2, 1, p0, p1, m1)
    rim(forward, -1, 2, p1, p2, m2)
    rim(forward, 0, 3, p2, None, m3)

    rows_of_moments = (
        both(m3, 0, 4, 5, 3, 1, 0), both(m3, 0, 4, 0, 3, -1),
        both(m2, 0, 4, 6, 1, 1, 0), both(m2, 0, 4, 1, 1, -1),
    )

    received(*deeper)

    @pl.when(whole[1][1])
    def _():
        def at(lowest, *refs):
            lax.fori_loop(0, 3, lambda k, _: (forward(*refs, k + lowest), 0)[1], 0, unroll=3)

        at(-5, p0, p1, m1)
        at(-4, p1, p2, m2)
        at(-3, p2, None, m3)

    received(*strips)
    left, right = mask_lanes(0, COLS, 64), mask_lanes(44, 44 + COLS, 64)

    def halo_strip(strip, tile, item, slot, place):
        by = slot * COLS
        low = pltpu.roll(got[tile, 0, place], (-by) % 128, 1)
        high = pltpu.roll(got[tile, 1, place], (44 - by) % 128, 1)
        return jnp.where(left, low, jnp.where(right, high, strip))

    def fill_strips(src, dst, first_item, count):
        for item in range(count):
            slot, place = (first_item + item) % SLOTS, (first_item + item) // SLOTS
            for tile in range(3):
                strip = dst[item, 8:16, :] if tile == 1 else own_strip(src, item, tile)
                dst[item, 8 * tile : 8 * tile + 8, :] = halo_strip(strip, tile, item, slot, place)

    fill_strips(p0, s0, 0, ITEMS)

    def strip_forward(src, dst, mom):
        f = {q: shift_strip(src[POST[q]], *LINKS[q]) for q in range(Q)}
        rho, *u = moments(f, s0[DRAG])
        for item, value in enumerate((rho, *u)):
            mom[item] = value
        if dst is not None:
            post = relax(f, rho, u, s0[SOLID])
            for q in range(Q):
                dst[POST[q]] = post[q]

    for item in range(4):
        k0[item, 8:16, :] = own_strip(m0, item, 1)
    strip_forward(s0, s1, k1)
    strip_forward(s1, s2, k2)
    strip_forward(s2, None, k3)
    for item in range(4):
        low, high = slice(3 * item, 3 * item + 3), slice(12 + item, 13 + item)
        edges[1, low, :], edges[1, high, :] = k3[item, 13:16, :], k2[item, 14:15, :]
        edges[0, low, :], edges[0, high, :] = k3[item, 8:11, :], k2[item, 9:10, :]
    strip_moments = [
        send(edges.at[(dx + 1) // 2], got_edges.at[(1 - dx) // 2], dx, 0, which)
        for dx, which in ((1, 0), (-1, None))
    ]

    def strip_backward(src, mom):
        inc = {q: shift_strip(src[ADJ[q]], *[-c for c in LINKS[q]]) for q in range(Q)}
        rho, *u = [mom[item] for item in range(4)]
        return pull(inc, rho, u, s0[DRAG], s0[SOLID])

    def strip_middle(src, dst, mom):
        out, back = strip_backward(src, mom)
        for q in range(Q):
            dst[ADJ[q]] = out[q]
        back_strip[...] = back if mom is k3 else back_strip[...] + back

    rows(middle, 1, 7, q0, q1, m3)
    rows(middle, 2, 6, q1, q2, m2)
    rows(middle, 3, 5, q2, q3, m1)

    def final(row, _):
        out, back = backward(q3, None, m0, row)
        there = pl.ds(row, 8, stride=8)
        for q in range(Q):
            out_ref[q, there, :] = out[q]
        grad_ref[there, :] = row_at_sum(row) + back
        return 0

    def row_at_sum(row):
        return sums[pl.ds(pl.multiple_of((row + 8) * 8, 8), 8), :]

    def last_rows(low, high):
        lax.fori_loop(low, high, final, 0, unroll=high - low)

    received(*adjoints)
    rim(middle, 0, 1, q0, q1, m3)
    rim(middle, 1, 2, q1, q2, m2)
    rim(middle, 2, 3, q2, q3, m1)
    last_rows(3, 5)
    fill_strips(q0, t0, ITEMS, Q)

    received(*rows_of_moments, *strip_moments)

    def take_edges(side, wide, thin):
        for item in range(4):
            low, high = slice(3 * item, 3 * item + 3), slice(12 + item, 13 + item)
            k3[item, wide, :], k2[item, thin, :] = got_edges[side, low, :], got_edges[side, high, :]

    pl.when(whole[0][1])(lambda: take_edges(0, slice(5, 8), slice(6, 7)))
    take_edges(1, slice(16, 19), slice(17, 18))
    rim(middle, -3, 0, q0, q1, m3)
    strip_middle(t0, t1, k3)
    rim(middle, -2, 1, q1, q2, m2)
    strip_middle(t1, t2, k2)
    rim(middle, -1, 2, q2, q3, m1)
    strip_middle(t2, t3, k1)
    strip_out, strip_back = strip_backward(t3, k0)
    for q in range(Q):
        t1[ADJ[q], 8:16, :] = strip_out[q][8:16]
    back_strip[8:16, :] = back_strip[8:16, :] + strip_back[8:16]
    last_rows(0, 3)
    last_rows(5, 8)

    edge_low, edge_high = mask_lanes(0, COLS, 128), mask_lanes(128 - COLS, 128, 128)

    def merge(ref, strip):
        for k, lane, chosen in ((0, 6, edge_low), (4, 70, edge_low), (3, 38 - 122, edge_high), (7, 102 - 122, edge_high)):
            here = slice(8 * k, 8 * k + 8)
            ref[here, :] = jnp.where(chosen, pltpu.roll(strip, (-lane) % 128, 1), ref[here, :])

    for q in range(Q):
        merge(out_ref.at[q], t1[ADJ[q], 8:16, :])
    merge(grad_ref, back_strip[8:16, :])

    sent(*copies)


def to_tiles(a):
    lead = a.shape[:-3]
    n = len(lead)
    a = a.reshape(*lead, 2, 8, 4, 128)
    a = a.transpose(*range(n), n, n + 2, n + 1, n + 3)
    return a.reshape(*lead, 64, 128)


def from_tiles(a):
    lead = a.shape[:-2]
    n = len(lead)
    a = a.reshape(*lead, 2, 4, 8, 128)
    a = a.transpose(*range(n), n, n + 2, n + 1, n + 3)
    return a.reshape(*lead, 2, 8, 512)


def solution(mesh):
    n_gx, n_gy = mesh.shape["gx"], mesh.shape["gy"]

    def local(start, final_adjoint, resist, mask):
        any_space = pl.BlockSpec(memory_space=pl.ANY)
        vmem = pl.BlockSpec(memory_space=pltpu.VMEM)
        buf = lambda *shape: pltpu.VMEM(shape, F32)
        out, grad = pl.pallas_call(
            functools.partial(kernel, n_gx, n_gy),
            out_shape=(
                pltpu.VMEM((Q, 64, 128), F32),
                pltpu.VMEM((64, 128), F32),
            ),
            in_specs=[any_space] * 4,
            out_specs=[vmem, vmem],
            scratch_shapes=[
                buf(Q, 64, 128), buf(Q, 64, 128), buf(64, 128), pltpu.VMEM((64, 128), jnp.int32),
                buf(ITEMS, 192, 128), buf(ITEMS, 192, 128), buf(ITEMS, 192, 128),
                buf(Q, 192, 128), buf(Q, 192, 128), buf(Q, 192, 128), buf(Q, 192, 128),
                buf(4, 192, 128), buf(4, 192, 128), buf(4, 192, 128), buf(4, 192, 128), buf(192, 128),
                buf(ITEMS, 24, 128), buf(ITEMS, 24, 128), buf(ITEMS, 24, 128),
                buf(Q, 24, 128), buf(Q, 24, 128), buf(Q, 24, 128), buf(Q, 24, 128),
                buf(4, 24, 128), buf(4, 24, 128), buf(4, 24, 128), buf(4, 24, 128), buf(24, 128),
                buf(2, PACK, 8, 128), buf(3, 2, PACK, 8, 128), buf(2, 16, 128), buf(2, 16, 128),
                pltpu.SemaphoreType.DMA((4,)),
                pltpu.SemaphoreType.DMA((32,)),
                pltpu.SemaphoreType.DMA((32,)),
            ],
            compiler_params=pltpu.CompilerParams(
                collective_id=0, has_side_effects=True, vmem_limit_bytes=48 * 2**20
            ),
        )(*[pltpu.with_memory_space_constraint(to_tiles(a), pltpu.HBM) for a in (start, final_adjoint, resist, mask)])
        return from_tiles(out), from_tiles(grad)

    return jax.shard_map(
        local,
        mesh=mesh,
        in_specs=(
            P(None, None, "gx", "gy"),
            P(None, None, "gx", "gy"),
            P(None, "gx", "gy"),
            P(None, "gx", "gy"),
        ),
        out_specs=(P(None, None, "gx", "gy"), P(None, "gx", "gy")),
        check_vma=False,
    )
```

```python
import functools

import jax
import jax.numpy as jnp
from jax import lax
from jax.experimental import pallas as pl
from jax.experimental.pallas import tpu as pltpu
from jax.sharding import PartitionSpec as P

MESH = pl.DeviceIdType.MESH
F32 = jnp.float32
OMEGA = 1.25
KEEP = 1.0 - OMEGA

LINKS = [
    (0, 0, 0),
    (1, 0, 0), (-1, 0, 0), (0, 1, 0), (0, -1, 0), (0, 0, 1), (0, 0, -1),
    (1, 1, 0), (-1, -1, 0), (1, -1, 0), (-1, 1, 0),
    (1, 0, 1), (-1, 0, -1), (1, 0, -1), (-1, 0, 1),
    (0, 1, 1), (0, -1, -1), (0, 1, -1), (0, -1, 1),
]
Q = 19
UP = [1, 7, 9, 11, 13]
FLAT = [0, 3, 4, 5, 6, 15, 16, 17, 18]
DOWN = [2, 8, 10, 12, 14]
DRAG, SOLID, ITEMS = 19, 20, 21
ADJ = POST = {q: k for k, q in enumerate(UP + FLAT + DOWN)}

ROWS = 8
COLS = 6
SLOTS = 10
PACK = 4


def mask_lanes(low, high, period):
    lane = lax.broadcasted_iota(jnp.int32, (8, 128), 1) % period
    return (lane >= low) & (lane < high)


def row_at(ref, item, row):
    return ref[item, pl.ds(pl.multiple_of((row + 8) * 8, 8), 8), :]


def set_row(ref, item, row, value):
    ref[item, pl.ds(pl.multiple_of((row + 8) * 8, 8), 8), :] = value


def shift_row(value, dy, dz):
    if dz:
        value = pltpu.roll(value, 4, 0)
    if dy:
        lane = lax.broadcasted_iota(jnp.int32, (8, 128), 1)
        moved = pltpu.roll(value, dy % 128, 1)
        beside = pltpu.roll(moved, dy % 8, 0)
        value = jnp.where(lane == (0 if dy > 0 else 127), beside, moved)
    return value


def shift_strip(value, dx, dy, dz):
    if dx:
        value = pltpu.roll(value, dx % 24, 0)
    turn = (dy + 64 * abs(dz)) % 128
    if turn:
        value = pltpu.roll(value, turn, 1)
    return value


def moments(f, drag):
    total = {}
    diff = {}
    for q in range(1, Q, 2):
        total[q] = f[q] + f[q + 1]
        diff[q] = f[q] - f[q + 1]
    rho = f[0] + ((total[1] + total[3]) + (total[5] + total[7])) + (
        (total[9] + total[11]) + (total[13] + (total[15] + total[17]))
    )
    scale = drag / rho
    ux = ((diff[1] + diff[7]) + (diff[9] + diff[11]) + diff[13]) * scale
    uy = ((diff[3] + diff[7]) + (diff[15] - diff[9]) + diff[17]) * scale
    uz = ((diff[5] + diff[11]) + (diff[15] - diff[13]) - diff[17]) * scale
    return ux, uy, uz, rho


def along(vec, q):
    out = None
    for part, c in zip(vec, LINKS[q]):
        if c:
            if out is None:
                out = part
            else:
                out = out + part if c > 0 else out - part
    return out


def relax(f, rho, u, solid):
    w2 = rho * (OMEGA / 36.0)
    b = [x * (w2 * 3.0) for x in u]
    h = [x * 1.5 for x in u]
    base = w2 - (u[0] * b[0] + u[1] * b[1] + u[2] * b[2]) * 0.5
    blocked = solid > 0.5
    post = {}
    post[0] = jnp.where(blocked, f[0], KEEP * f[0] + 12.0 * base)
    twice = base + base
    for q in range(1, Q, 2):
        cb, ch = along(b, q), along(h, q)
        if q < 7:
            cb = cb + cb
            even = twice + cb * ch
        else:
            even = base + cb * ch
        post[q] = jnp.where(blocked, f[q + 1], KEEP * f[q] + (even + cb))
        post[q + 1] = jnp.where(blocked, f[q], KEEP * f[q + 1] + (even - cb))
    return post


def pull(inc, rho, u, drag, solid):
    ux, uy, uz = u
    blocked = solid > 0.5
    s, d = {}, {}
    for q in range(1, Q, 2):
        s[q] = inc[q] + inc[q + 1]
        d[q] = inc[q] - inc[q + 1]
    sxy, sxz, syz = s[7] + s[9], s[11] + s[13], s[15] + s[17]
    kxx = (s[1] + s[1]) + sxy + sxz
    kyy = (s[3] + s[3]) + sxy + syz
    kzz = (s[5] + s[5]) + sxz + syz
    kxy, kxz, kyz = s[7] - s[9], s[11] - s[13], s[15] - s[17]
    k0 = 12.0 * inc[0] + 2.0 * (s[1] + s[3] + s[5]) + (sxy + sxz + syz)
    kx = (d[1] + d[1]) + (d[7] + d[9]) + (d[11] + d[13])
    ky = (d[3] + d[3]) + (d[7] - d[9]) + (d[15] + d[17])
    kz = (d[5] + d[5]) + (d[11] - d[13]) + (d[15] - d[17])
    wk = OMEGA / 36.0
    vx = kxx * ux + kxy * uy + kxz * uz
    vy = kxy * ux + kyy * uy + kyz * uz
    vz = kxz * ux + kyz * uy + kzz * uz
    gx = 3.0 * (kx - k0 * ux) + 9.0 * vx
    gy = 3.0 * (ky - k0 * uy) + 9.0 * vy
    gz = 3.0 * (kz - k0 * uz) + 9.0 * vz
    uu = ux * ux + uy * uy + uz * uz
    uku = ux * vx + uy * vy + uz * vz
    grho = wk * (k0 + 1.5 * (k0 * uu) - 4.5 * uku)
    ku = kx * ux + ky * uy + kz * uz
    du = 3.0 * (ku - k0 * uu) + 9.0 * uku
    scale = wk * drag
    g = (gx * scale, gy * scale, gz * scale)
    back = jnp.where(blocked, 0.0, (rho * du) * (-scale))
    out = {0: jnp.where(blocked, inc[0], KEEP * inc[0] + grho)}
    for q in range(1, Q, 2):
        cg = along(g, q)
        out[q] = jnp.where(blocked, inc[q + 1], KEEP * inc[q] + (grho + cg))
        out[q + 1] = jnp.where(blocked, inc[q], KEEP * inc[q + 1] + (grho - cg))
    return out, back


def kernel(
    n_gx, n_gy, start_hbm, adj_hbm, resist_hbm, mask_hbm, out_ref, grad_ref,
    start, adj, resist, mask, p0, p1, p2, q0, q1, q2, q3, m0, m1, m2, m3, sums,
    s0, s1, s2, t0, t1, t2, t3, k0, k1, k2, k3, back_strip, packs, got, edges, got_edges, relay, got_relay,
    load_sem, send_sem, recv_sem,
):
    gx, gy = lax.axis_index("gx"), lax.axis_index("gy")

    def device(dx, dy):
        return (lax.rem(gx + dx + n_gx, n_gx), lax.rem(gy + dy + n_gy, n_gy))

    around = [(-1, 0), (1, 0), (0, -1), (0, 1)]
    barrier = pltpu.get_barrier_semaphore()
    for dx, dy in around:
        pl.semaphore_signal(barrier, inc=1, device_id=device(dx, dy), device_id_type=MESH)

    loads = [
        pltpu.make_async_copy(src, dst, load_sem.at[k])
        for k, (src, dst) in enumerate(
            ((start_hbm, start), (resist_hbm, resist), (mask_hbm, mask), (adj_hbm, adj))
        )
    ]
    for copy in loads:
        copy.start()
    for copy in loads[:3]:
        copy.wait()

    def first(k, _):
        here = pl.ds(pl.multiple_of(k * 8, 8), 8)
        there = pl.ds(64 + k, 8, stride=8)
        f = {q: start[q, here, :] for q in range(Q)}
        drag = 1.0 / (1.0 + resist[here, :])
        solid = mask[here, :].astype(F32)
        *u, rho = moments(f, drag)
        post = relax(f, rho, u, solid)
        for q in range(Q):
            p0[POST[q], there, :] = post[q]
        p0[DRAG, there, :] = drag
        p0[SOLID, there, :] = solid
        for item, value in enumerate((*u, rho)):
            m0[item, there, :] = value
        return 0

    lax.fori_loop(0, 8, first, 0, unroll=4)
    loads[3].wait()

    def turn(k, _):
        here = pl.ds(pl.multiple_of(k * 8, 8), 8)
        there = pl.ds(64 + k, 8, stride=8)
        for q in range(Q):
            q0[ADJ[q], there, :] = adj[q, here, :]
        return 0

    lax.fori_loop(0, 8, turn, 0)

    low0, low1, low2 = mask_lanes(0, 32, 128), mask_lanes(64, 96, 128), mask_lanes(32, 64, 128)

    def own_strip(src, item, tile):
        def part(k, by):
            return pltpu.roll(src[item, pl.ds(tile * 64 + k, 8, stride=8), :], by, 1)

        return jnp.where(
            low0, part(0, 6), jnp.where(low1, part(4, 70), jnp.where(low2, part(3, 44), part(7, 108)))
        )

    sides = [[None] * PACK, [None] * PACK]
    for item in range(ITEMS + Q):
        slot, place = item % SLOTS, item // SLOTS
        src, dst, index = (p0, s0, item) if item < ITEMS else (q0, t0, item - ITEMS)
        strip = own_strip(src, index, 1)
        dst[index, 8:16, :] = strip
        chosen = mask_lanes(slot * COLS, slot * COLS + COLS, 64)
        for side, lane in ((0, 6), (1, 38)):
            moved = pltpu.roll(strip, (slot * COLS - lane) % 128, 1)
            old = sides[side][place]
            sides[side][place] = moved if old is None else jnp.where(chosen, moved, old)
    for side in range(2):
        for place in range(PACK):
            packs[side, place] = sides[side][place]


    pl.semaphore_wait(barrier, len(around))

    copies = []
    first_x, last_x = gx == 0, gx == n_gx - 1
    paired_up = lax.rem(gx, 2) == 0
    paired_down = jnp.logical_not(paired_up)
    along_x = jnp.logical_or(lax.rem(gx, 4) == 1, lax.rem(gx, 4) == 2)
    along_z = jnp.logical_not(along_x)

    def make(src, dst, dx, dy, sent_if=None, got_if=None):
        k = len(copies)
        copy = pltpu.make_async_remote_copy(
            src_ref=src, dst_ref=dst, send_sem=send_sem.at[k], recv_sem=recv_sem.at[k],
            device_id=device(dx, dy), device_id_type=MESH,
        )
        copies.append((copy, sent_if, got_if))
        return copies[-1]

    def only_if(condition, action):
        if condition is None:
            action()
        else:
            pl.when(condition)(action)

    def start(*batch):
        for copy, sent_if, _ in batch:
            only_if(sent_if, copy.start)

    def received(*batch):
        for copy, _, got_if in batch:
            only_if(got_if, copy.wait_recv)

    def received_near(from_low, from_high):
        pl.when(paired_up)(lambda: received(*from_high))
        pl.when(paired_down)(lambda: received(*from_low))

    def received_far(from_low, from_high):
        pl.when(paired_up)(lambda: received(*from_low))
        pl.when(paired_down)(lambda: received(*from_high))

    def start_near(to_high, to_low):
        pl.when(paired_up)(lambda: start(*to_high))
        pl.when(paired_down)(lambda: start(*to_low))

    def start_far(to_high, to_low):
        pl.when(paired_up)(lambda: start(*to_low))
        pl.when(paired_down)(lambda: start(*to_high))

    def span(ref, low, high, row, count):
        return ref.at[pl.ds(low, high - low), pl.ds((row + 8) * 8, count * 8), :]

    def halo(ref, low, high, row, count, dx, *conditions):
        there = span(ref, low, high, row - 8 * dx, count)
        return make(span(ref, low, high, row, count), there, dx, 0, *conditions)

    deep, shallow = (last_x, first_x), (jnp.logical_not(last_x), jnp.logical_not(first_x))

    strips = [make(packs.at[(dy + 1) // 2], got.at[1, (1 - dy) // 2], 0, dy) for dy in (-1, 1)]
    posts_low = (
        halo(p0, 0, 19, 7, 1, 1), halo(p0, 19, 21, 5, 3, 1), halo(p0, 0, 14, 6, 1, 1), halo(p0, 0, 5, 5, 1, 1),
    )
    posts_high = (
        halo(p0, 0, 19, 0, 1, -1), halo(p0, 19, 21, 0, 3, -1), halo(p0, 5, 19, 1, 1, -1), halo(p0, 14, 19, 2, 1, -1),
    )
    deeper = [
        halo(p0, 14, 19, 6, 1, 1, *deep), halo(p0, 5, 19, 5, 1, 1, *deep), halo(p0, 19, 21, 3, 2, 1, *deep),
        halo(p0, 0, 19, 4, 1, 1, *deep), halo(p0, 0, 14, 3, 1, 1, *deep), halo(p0, 0, 5, 2, 1, 1, *deep),
    ]
    adj_low = (halo(q0, 0, 19, 7, 1, 1), halo(q0, 0, 19, 6, 1, 1), halo(q0, 5, 19, 5, 1, 1), halo(q0, 14, 19, 4, 1, 1))
    adj_high = (halo(q0, 0, 19, 0, 1, -1), halo(q0, 0, 19, 1, 1, -1), halo(q0, 0, 14, 2, 1, -1), halo(q0, 0, 5, 3, 1, -1))
    mom_low = (halo(m3, 0, 3, 5, 3, 1, *shallow), halo(m2, 0, 3, 6, 1, 1, *shallow))
    mom_high = (halo(m3, 0, 3, 0, 3, -1), halo(m2, 0, 3, 1, 1, -1))
    relay_low = make(relay.at[1], got_relay.at[0], 1, 0, *shallow)
    relay_high = make(relay.at[0], got_relay.at[1], -1, 0)
    relay_deep = make(got.at[1], got.at[0], 1, 0, *deep)
    edge_low = make(edges.at[1], got_edges.at[0], 1, 0, *shallow)
    edge_high = make(edges.at[0], got_edges.at[1], -1, 0)

    start(*strips)
    start_far(posts_low, posts_high)
    start_near(posts_low, posts_high)
    start(*deeper)

    def forward(src, dst, mom, row):
        f = {
            q: shift_row(row_at(src, POST[q], row - LINKS[q][0]), LINKS[q][1], LINKS[q][2])
            for q in range(Q)
        }
        *u, rho = moments(f, row_at(p0, DRAG, row))
        for item, value in enumerate((*u, rho)):
            set_row(mom, item, row, value)
        if dst is not None:
            post = relax(f, rho, u, row_at(p0, SOLID, row))
            for q in range(Q):
                set_row(dst, POST[q], row, post[q])

    def backward(src, dst, mom, row):
        inc = {
            q: shift_row(row_at(src, ADJ[q], row + LINKS[q][0]), -LINKS[q][1], LINKS[q][2])
            for q in range(Q)
        }
        *u, rho = [row_at(mom, item, row) for item in range(4)]
        return pull(inc, rho, u, row_at(p0, DRAG, row), row_at(p0, SOLID, row))

    def middle(src, dst, mom, row):
        out, back = backward(src, dst, mom, row)
        for q in range(Q):
            set_row(dst, ADJ[q], row, out[q])
        place = pl.ds(pl.multiple_of((row + 8) * 8, 8), 8)
        sums[place, :] = back if mom is m3 else sums[place, :] + back

    def line(body, low, high, *refs):
        def one(k, _):
            body(*refs, jnp.where(paired_up, 7 - low - k, low + k))
            return 0

        lax.fori_loop(0, high - low, one, 0, unroll=min(4, high - low))

    def final(row):
        out, back = backward(q3, None, m0, row)
        there = pl.ds(row, 8, stride=8)
        for q in range(Q):
            out_ref[q, there, :] = out[q]
        grad_ref[there, :] = sums[pl.ds(pl.multiple_of((row + 8) * 8, 8), 8), :] + back

    line(forward, 1, 7, p0, p1, m1)
    line(forward, 2, 6, p1, p2, m2)
    line(forward, 3, 5, p2, None, m3)

    start_near(adj_low, adj_high)
    pl.when(along_x)(lambda: start_far(adj_low[:1], adj_high[:1]))

    received(*strips)
    first_half = lax.broadcasted_iota(jnp.int32, (8, 128), 0) < 4
    for place in range(PACK):
        low, high = got[1, 0, place], got[1, 1, place]
        relay[1, place] = jnp.where(first_half, pltpu.roll(low, 4, 0), high)
        relay[0, place] = jnp.where(first_half, low, pltpu.roll(high, 4, 0))
    start(relay_low, relay_high, relay_deep)
    pl.when(along_x)(lambda: start_far(adj_low[1:], adj_high[1:]))

    received_near(posts_low, posts_high)
    line(forward, -2, 1, p0, p1, m1)
    line(forward, -1, 2, p1, p2, m2)
    line(forward, 0, 3, p2, None, m3)
    start_near(mom_low, mom_high)
    left, right = mask_lanes(0, COLS, 64), mask_lanes(44, 44 + COLS, 64)
    near, far = jnp.where(paired_up, 2, 0), jnp.where(paired_up, 0, 2)

    def fill_strips(src, dst, first_item, count, tile):
        for item in range(count):
            slot, place = (first_item + item) % SLOTS, (first_item + item) // SLOTS
            by = slot * COLS
            here = pl.ds(pl.multiple_of(8 * tile, 8), 8)
            strip = dst[item, 8:16, :] if isinstance(tile, int) else own_strip(src, item, tile)
            low = pltpu.roll(got[tile, 0, place], (-by) % 128, 1)
            high = pltpu.roll(got[tile, 1, place], (44 - by) % 128, 1)
            dst[item, here, :] = jnp.where(left, low, jnp.where(right, high, strip))

    def take_low():
        received(relay_low)
        for place in range(PACK):
            both_sides = got_relay[0, place]
            got[0, 0, place], got[0, 1, place] = pltpu.roll(both_sides, 4, 0), both_sides

    def take_high():
        received(relay_high)
        for place in range(PACK):
            both_sides = got_relay[1, place]
            got[2, 0, place], got[2, 1, place] = both_sides, pltpu.roll(both_sides, 4, 0)

    def strip_forward(src, dst, mom):
        f = {q: shift_strip(src[POST[q]], *LINKS[q]) for q in range(Q)}
        *u, rho = moments(f, s0[DRAG])
        for item, value in enumerate((*u, rho)):
            mom[item] = value
        if dst is not None:
            post = relax(f, rho, u, s0[SOLID])
            for q in range(Q):
                dst[POST[q]] = post[q]

    for item in range(4):
        k0[item, 8:16, :] = own_strip(m0, item, 1)

    def strips_forward():
        strip_forward(s0, s1, k1)
        strip_forward(s1, s2, k2)
        strip_forward(s2, None, k3)

    def put_edges(side, wide, thin):
        for item in range(3):
            edges[side, 3 * item : 3 * item + 3, :] = k3[item, wide, :]
            edges[side, 9 + item : 10 + item, :] = k2[item, thin, :]

    def put_high():
        put_edges(1, slice(13, 16), slice(14, 15))
        start(edge_low)

    def put_low():
        put_edges(0, slice(8, 11), slice(9, 10))
        start(edge_high)

    def strip_backward(src, mom):
        inc = {q: shift_strip(src[ADJ[q]], *[-c for c in LINKS[q]]) for q in range(Q)}
        *u, rho = [mom[item] for item in range(4)]
        return pull(inc, rho, u, s0[DRAG], s0[SOLID])

    def strip_middle(src, dst, mom):
        out, back = strip_backward(src, mom)
        for q in range(Q):
            dst[ADJ[q]] = out[q]
        back_strip[...] = back if mom is k3 else back_strip[...] + back

    fill_strips(p0, s0, 0, ITEMS, 1)
    fill_strips(q0, t0, ITEMS, Q, 1)

    received_far(posts_low, posts_high)
    pl.when(along_z)(lambda: start_far(adj_low, adj_high))
    line(forward, 7, 10, p0, p1, m1)
    line(forward, 6, 9, p1, p2, m2)
    line(forward, 5, 8, p2, None, m3)
    start_far(mom_low, mom_high)

    pl.when(paired_up)(take_high)
    pl.when(paired_down)(take_low)
    fill_strips(p0, s0, 0, ITEMS, near)
    pl.when(paired_down)(take_high)

    @pl.when(jnp.logical_and(paired_up, shallow[1]))
    def _():
        take_low()

    pl.when(shallow[1])(lambda: fill_strips(p0, s0, 0, ITEMS, far))
    strips_forward()
    put_high()
    pl.when(shallow[1])(put_low)

    received_near(adj_low, adj_high)
    received_near(mom_low, mom_high)
    line(middle, -3, 5, q0, q1, m3)
    line(middle, -2, 4, q1, q2, m2)
    line(middle, -1, 3, q2, q3, m1)
    line(final, 0, 2)
    fill_strips(q0, t0, ITEMS, Q, near)

    line(middle, 5, 7, q0, q1, m3)
    line(middle, 4, 6, q1, q2, m2)
    line(middle, 3, 5, q2, q3, m1)
    line(final, 2, 4)

    received(*deeper, relay_deep)

    @pl.when(first_x)
    def _():
        def at(lowest, *refs):
            lax.fori_loop(0, 3, lambda k, _: (forward(*refs, k + lowest), 0)[1], 0, unroll=3)

        at(-5, p0, p1, m1)
        at(-4, p1, p2, m2)
        at(-3, p2, None, m3)
        fill_strips(p0, s0, 0, ITEMS, far)
        strips_forward()
        put_low()

    received_far(adj_low, adj_high)
    fill_strips(q0, t0, ITEMS, Q, far)

    received_far(mom_low, mom_high)
    received(edge_low, edge_high)

    def take_edges(side, wide, thin):
        for item in range(3):
            k3[item, wide, :] = got_edges[side, 3 * item : 3 * item + 3, :]
            k2[item, thin, :] = got_edges[side, 9 + item : 10 + item, :]

    pl.when(shallow[1])(lambda: take_edges(0, slice(5, 8), slice(6, 7)))
    take_edges(1, slice(16, 19), slice(17, 18))
    line(middle, 7, 11, q0, q1, m3)
    strip_middle(t0, t1, k3)
    line(middle, 6, 10, q1, q2, m2)
    strip_middle(t1, t2, k2)
    line(middle, 5, 9, q2, q3, m1)
    strip_middle(t2, t3, k1)
    strip_out, strip_back = strip_backward(t3, k0)
    for q in range(Q):
        t1[ADJ[q], 8:16, :] = strip_out[q][8:16]
    back_strip[8:16, :] = back_strip[8:16, :] + strip_back[8:16]
    line(final, 4, 8)

    first_cols, last_cols = mask_lanes(0, COLS, 128), mask_lanes(128 - COLS, 128, 128)

    def merge(ref, strip):
        for k, lane, chosen in ((0, 6, first_cols), (4, 70, first_cols), (3, 38 - 122, last_cols), (7, 102 - 122, last_cols)):
            here = slice(8 * k, 8 * k + 8)
            ref[here, :] = jnp.where(chosen, pltpu.roll(strip, (-lane) % 128, 1), ref[here, :])

    for q in range(Q):
        merge(out_ref.at[q], t1[ADJ[q], 8:16, :])
    merge(grad_ref, back_strip[8:16, :])

    for copy, sent_if, _ in copies:
        only_if(sent_if, copy.wait_send)


def to_tiles(a):
    lead = a.shape[:-3]
    n = len(lead)
    a = a.reshape(*lead, 2, 8, 4, 128)
    a = a.transpose(*range(n), n, n + 2, n + 1, n + 3)
    return a.reshape(*lead, 64, 128)


def from_tiles(a):
    lead = a.shape[:-2]
    n = len(lead)
    a = a.reshape(*lead, 2, 4, 8, 128)
    a = a.transpose(*range(n), n, n + 2, n + 1, n + 3)
    return a.reshape(*lead, 2, 8, 512)


def solution(mesh):
    n_gx, n_gy = mesh.shape["gx"], mesh.shape["gy"]

    def local(start, final_adjoint, resist, mask):
        any_space = pl.BlockSpec(memory_space=pl.ANY)
        vmem = pl.BlockSpec(memory_space=pltpu.VMEM)
        buf = lambda *shape: pltpu.VMEM(shape, F32)
        out, grad = pl.pallas_call(
            functools.partial(kernel, n_gx, n_gy),
            out_shape=(
                pltpu.VMEM((Q, 64, 128), F32),
                pltpu.VMEM((64, 128), F32),
            ),
            in_specs=[any_space] * 4,
            out_specs=[vmem, vmem],
            scratch_shapes=[
                buf(Q, 64, 128), buf(Q, 64, 128), buf(64, 128), pltpu.VMEM((64, 128), jnp.int32),
                buf(ITEMS, 192, 128), buf(ITEMS, 192, 128), buf(ITEMS, 192, 128),
                buf(Q, 192, 128), buf(Q, 192, 128), buf(Q, 192, 128), buf(Q, 192, 128),
                buf(4, 192, 128), buf(4, 192, 128), buf(4, 192, 128), buf(4, 192, 128), buf(192, 128),
                buf(ITEMS, 24, 128), buf(ITEMS, 24, 128), buf(ITEMS, 24, 128),
                buf(Q, 24, 128), buf(Q, 24, 128), buf(Q, 24, 128), buf(Q, 24, 128),
                buf(4, 24, 128), buf(4, 24, 128), buf(4, 24, 128), buf(4, 24, 128), buf(24, 128),
                buf(2, PACK, 8, 128), buf(3, 2, PACK, 8, 128), buf(2, 16, 128), buf(2, 16, 128),
                buf(2, PACK, 8, 128), buf(2, PACK, 8, 128),
                pltpu.SemaphoreType.DMA((4,)),
                pltpu.SemaphoreType.DMA((38,)),
                pltpu.SemaphoreType.DMA((38,)),
            ],
            compiler_params=pltpu.CompilerParams(
                collective_id=0, has_side_effects=True, vmem_limit_bytes=48 * 2**20
            ),
        )(*[pltpu.with_memory_space_constraint(to_tiles(a), pltpu.HBM) for a in (start, final_adjoint, resist, mask)])
        return from_tiles(out), from_tiles(grad)

    return jax.shard_map(
        local,
        mesh=mesh,
        in_specs=(
            P(None, None, "gx", "gy"),
            P(None, None, "gx", "gy"),
            P(None, "gx", "gy"),
            P(None, "gx", "gy"),
        ),
        out_specs=(P(None, None, "gx", "gy"), P(None, "gx", "gy")),
        check_vma=False,
    )
```

```python
import functools

import jax
import jax.numpy as jnp
from jax import lax
from jax.experimental import pallas as pl
from jax.experimental.pallas import tpu as pltpu
from jax.sharding import PartitionSpec as P

MESH = pl.DeviceIdType.MESH
F32 = jnp.float32
OMEGA = 1.25
KEEP = 1.0 - OMEGA

LINKS = [
    (0, 0, 0),
    (1, 0, 0), (-1, 0, 0), (0, 1, 0), (0, -1, 0), (0, 0, 1), (0, 0, -1),
    (1, 1, 0), (-1, -1, 0), (1, -1, 0), (-1, 1, 0),
    (1, 0, 1), (-1, 0, -1), (1, 0, -1), (-1, 0, 1),
    (0, 1, 1), (0, -1, -1), (0, 1, -1), (0, -1, 1),
]
Q = 19
UP = [1, 7, 9, 11, 13]
FLAT = [0, 3, 4, 5, 6, 15, 16, 17, 18]
DOWN = [2, 8, 10, 12, 14]
DRAG, SOLID, ITEMS = 19, 20, 21
ADJ = POST = {q: k for k, q in enumerate(UP + FLAT + DOWN)}

ROWS = 8
COLS = 6
SLOTS = 10
PACK = 4


def mask_lanes(low, high, period):
    lane = lax.broadcasted_iota(jnp.int32, (8, 128), 1) % period
    return (lane >= low) & (lane < high)


def row_at(ref, item, row):
    return ref[item, pl.ds(pl.multiple_of((row + 8) * 8, 8), 8), :]


def set_row(ref, item, row, value):
    ref[item, pl.ds(pl.multiple_of((row + 8) * 8, 8), 8), :] = value


def shift_row(value, dy, dz):
    if dz:
        value = pltpu.roll(value, 4, 0)
    if dy:
        lane = lax.broadcasted_iota(jnp.int32, (8, 128), 1)
        moved = pltpu.roll(value, dy % 128, 1)
        beside = pltpu.roll(moved, dy % 8, 0)
        value = jnp.where(lane == (0 if dy > 0 else 127), beside, moved)
    return value


def shift_strip(value, dx, dy, dz):
    if dx:
        value = pltpu.roll(value, dx % 24, 0)
    turn = (dy + 64 * abs(dz)) % 128
    if turn:
        value = pltpu.roll(value, turn, 1)
    return value


def moments(f, drag):
    total = {}
    diff = {}
    for q in range(1, Q, 2):
        total[q] = f[q] + f[q + 1]
        diff[q] = f[q] - f[q + 1]
    rho = f[0] + ((total[1] + total[3]) + (total[5] + total[7])) + (
        (total[9] + total[11]) + (total[13] + (total[15] + total[17]))
    )
    scale = drag / rho
    ux = ((diff[1] + diff[7]) + (diff[9] + diff[11]) + diff[13]) * scale
    uy = ((diff[3] + diff[7]) + (diff[15] - diff[9]) + diff[17]) * scale
    uz = ((diff[5] + diff[11]) + (diff[15] - diff[13]) - diff[17]) * scale
    return ux, uy, uz, rho


def along(vec, q):
    out = None
    for part, c in zip(vec, LINKS[q]):
        if c:
            if out is None:
                out = part
            else:
                out = out + part if c > 0 else out - part
    return out


def relax(f, rho, u, solid):
    w2 = rho * (OMEGA / 36.0)
    b = [x * (w2 * 3.0) for x in u]
    h = [x * 1.5 for x in u]
    base = w2 - (u[0] * b[0] + u[1] * b[1] + u[2] * b[2]) * 0.5
    blocked = solid > 0.5
    post = {}
    post[0] = jnp.where(blocked, f[0], KEEP * f[0] + 12.0 * base)
    twice = base + base
    for q in range(1, Q, 2):
        cb, ch = along(b, q), along(h, q)
        if q < 7:
            cb = cb + cb
            even = twice + cb * ch
        else:
            even = base + cb * ch
        post[q] = jnp.where(blocked, f[q + 1], KEEP * f[q] + (even + cb))
        post[q + 1] = jnp.where(blocked, f[q], KEEP * f[q + 1] + (even - cb))
    return post


def pull(inc, rho, u, drag, solid):
    ux, uy, uz = u
    blocked = solid > 0.5
    s, d = {}, {}
    for q in range(1, Q, 2):
        s[q] = inc[q] + inc[q + 1]
        d[q] = inc[q] - inc[q + 1]
    sxy, sxz, syz = s[7] + s[9], s[11] + s[13], s[15] + s[17]
    kxx = (s[1] + s[1]) + sxy + sxz
    kyy = (s[3] + s[3]) + sxy + syz
    kzz = (s[5] + s[5]) + sxz + syz
    kxy, kxz, kyz = s[7] - s[9], s[11] - s[13], s[15] - s[17]
    k0 = 12.0 * inc[0] + 2.0 * (s[1] + s[3] + s[5]) + (sxy + sxz + syz)
    kx = (d[1] + d[1]) + (d[7] + d[9]) + (d[11] + d[13])
    ky = (d[3] + d[3]) + (d[7] - d[9]) + (d[15] + d[17])
    kz = (d[5] + d[5]) + (d[11] - d[13]) + (d[15] - d[17])
    wk = OMEGA / 36.0
    vx = kxx * ux + kxy * uy + kxz * uz
    vy = kxy * ux + kyy * uy + kyz * uz
    vz = kxz * ux + kyz * uy + kzz * uz
    gx = 3.0 * (kx - k0 * ux) + 9.0 * vx
    gy = 3.0 * (ky - k0 * uy) + 9.0 * vy
    gz = 3.0 * (kz - k0 * uz) + 9.0 * vz
    uu = ux * ux + uy * uy + uz * uz
    uku = ux * vx + uy * vy + uz * vz
    grho = wk * (k0 + 1.5 * (k0 * uu) - 4.5 * uku)
    ku = kx * ux + ky * uy + kz * uz
    du = 3.0 * (ku - k0 * uu) + 9.0 * uku
    scale = wk * drag
    g = (gx * scale, gy * scale, gz * scale)
    back = jnp.where(blocked, 0.0, (rho * du) * (-scale))
    out = {0: jnp.where(blocked, inc[0], KEEP * inc[0] + grho)}
    for q in range(1, Q, 2):
        cg = along(g, q)
        out[q] = jnp.where(blocked, inc[q + 1], KEEP * inc[q] + (grho + cg))
        out[q + 1] = jnp.where(blocked, inc[q], KEEP * inc[q + 1] + (grho - cg))
    return out, back


def kernel(
    n_gx, n_gy, start_hbm, adj_hbm, resist_hbm, mask_hbm, out_ref, grad_ref,
    start, adj, resist, mask, p0, p1, p2, q0, q1, q2, q3, m0, m1, m2, m3, sums,
    s0, s1, s2, t0, t1, t2, t3, k0, k1, k2, k3, back_strip, packs, got, edges, got_edges, relay, got_relay,
    load_sem, send_sem, recv_sem,
):
    gx, gy = lax.axis_index("gx"), lax.axis_index("gy")

    def device(dx, dy):
        return (lax.rem(gx + dx + n_gx, n_gx), lax.rem(gy + dy + n_gy, n_gy))

    around = [(-1, 0), (1, 0), (0, -1), (0, 1)]
    barrier = pltpu.get_barrier_semaphore()
    for dx, dy in around:
        pl.semaphore_signal(barrier, inc=1, device_id=device(dx, dy), device_id_type=MESH)

    loads = [
        pltpu.make_async_copy(src, dst, load_sem.at[k])
        for k, (src, dst) in enumerate(
            ((start_hbm, start), (resist_hbm, resist), (mask_hbm, mask), (adj_hbm, adj))
        )
    ]
    for copy in loads:
        copy.start()
    for copy in loads[:3]:
        copy.wait()

    def first(k, _):
        here = pl.ds(pl.multiple_of(k * 8, 8), 8)
        there = pl.ds(64 + k, 8, stride=8)
        f = {q: start[q, here, :] for q in range(Q)}
        drag = 1.0 / (1.0 + resist[here, :])
        solid = mask[here, :].astype(F32)
        *u, rho = moments(f, drag)
        post = relax(f, rho, u, solid)
        for q in range(Q):
            p0[POST[q], there, :] = post[q]
        p0[DRAG, there, :] = drag
        p0[SOLID, there, :] = solid
        for item, value in enumerate((*u, rho)):
            m0[item, there, :] = value
        return 0

    lax.fori_loop(0, 8, first, 0, unroll=4)
    loads[3].wait()

    def turn(k, _):
        here = pl.ds(pl.multiple_of(k * 8, 8), 8)
        there = pl.ds(64 + k, 8, stride=8)
        for q in range(Q):
            q0[ADJ[q], there, :] = adj[q, here, :]
        return 0

    lax.fori_loop(0, 8, turn, 0)

    low0, low1, low2 = mask_lanes(0, 32, 128), mask_lanes(64, 96, 128), mask_lanes(32, 64, 128)

    def own_strip(src, item, tile):
        def part(k, by):
            return pltpu.roll(src[item, pl.ds(tile * 64 + k, 8, stride=8), :], by, 1)

        return jnp.where(
            low0, part(0, 6), jnp.where(low1, part(4, 70), jnp.where(low2, part(3, 44), part(7, 108)))
        )

    sides = [[None] * PACK, [None] * PACK]
    for item in range(ITEMS + Q):
        slot, place = item % SLOTS, item // SLOTS
        src, dst, index = (p0, s0, item) if item < ITEMS else (q0, t0, item - ITEMS)
        strip = own_strip(src, index, 1)
        dst[index, 8:16, :] = strip
        chosen = mask_lanes(slot * COLS, slot * COLS + COLS, 64)
        for side, lane in ((0, 6), (1, 38)):
            moved = pltpu.roll(strip, (slot * COLS - lane) % 128, 1)
            old = sides[side][place]
            sides[side][place] = moved if old is None else jnp.where(chosen, moved, old)
    for side in range(2):
        for place in range(PACK):
            packs[side, place] = sides[side][place]


    pl.semaphore_wait(barrier, len(around))

    copies = []
    first_x, last_x = gx == 0, gx == n_gx - 1
    paired_up = lax.rem(gx, 2) == 0
    paired_down = jnp.logical_not(paired_up)
    along_x = jnp.logical_or(lax.rem(gx, 4) == 1, lax.rem(gx, 4) == 2)
    along_z = jnp.logical_and(jnp.logical_not(along_x), jnp.logical_not(last_x))

    def make(src, dst, dx, dy, sent_if=None, got_if=None):
        k = len(copies)
        copy = pltpu.make_async_remote_copy(
            src_ref=src, dst_ref=dst, send_sem=send_sem.at[k], recv_sem=recv_sem.at[k],
            device_id=device(dx, dy), device_id_type=MESH,
        )
        copies.append((copy, sent_if, got_if))
        return copies[-1]

    def only_if(condition, action):
        if condition is None:
            action()
        else:
            pl.when(condition)(action)

    def start(*batch):
        for copy, sent_if, _ in batch:
            only_if(sent_if, copy.start)

    def received(*batch):
        for copy, _, got_if in batch:
            only_if(got_if, copy.wait_recv)

    def received_near(from_low, from_high):
        pl.when(paired_up)(lambda: received(*from_high))
        pl.when(paired_down)(lambda: received(*from_low))

    def received_far(from_low, from_high):
        pl.when(paired_up)(lambda: received(*from_low))
        pl.when(paired_down)(lambda: received(*from_high))

    def start_near(to_high, to_low):
        pl.when(paired_up)(lambda: start(*to_high))
        pl.when(paired_down)(lambda: start(*to_low))

    def start_far(to_high, to_low):
        pl.when(paired_up)(lambda: start(*to_low))
        pl.when(paired_down)(lambda: start(*to_high))

    def span(ref, low, high, row, count):
        return ref.at[pl.ds(low, high - low), pl.ds((row + 8) * 8, count * 8), :]

    def halo(ref, low, high, row, count, dx, *conditions):
        there = span(ref, low, high, row - 8 * dx, count)
        return make(span(ref, low, high, row, count), there, dx, 0, *conditions)

    deep, shallow = (last_x, first_x), (jnp.logical_not(last_x), jnp.logical_not(first_x))

    strips = [make(packs.at[(dy + 1) // 2], got.at[1, (1 - dy) // 2], 0, dy) for dy in (-1, 1)]
    posts_low = (
        halo(p0, 0, 19, 7, 1, 1), halo(p0, 19, 21, 5, 3, 1), halo(p0, 0, 14, 6, 1, 1), halo(p0, 0, 5, 5, 1, 1),
    )
    posts_high = (
        halo(p0, 0, 19, 0, 1, -1), halo(p0, 19, 21, 0, 3, -1), halo(p0, 5, 19, 1, 1, -1), halo(p0, 14, 19, 2, 1, -1),
    )
    deeper = [
        halo(p0, 14, 19, 6, 1, 1, *deep), halo(p0, 5, 19, 5, 1, 1, *deep), halo(p0, 19, 21, 3, 2, 1, *deep),
        halo(p0, 0, 19, 4, 1, 1, *deep), halo(p0, 0, 14, 3, 1, 1, *deep), halo(p0, 0, 5, 2, 1, 1, *deep),
    ]
    adj_low = (halo(q0, 0, 19, 7, 1, 1), halo(q0, 0, 19, 6, 1, 1), halo(q0, 5, 19, 5, 1, 1), halo(q0, 14, 19, 4, 1, 1))
    adj_high = (halo(q0, 0, 19, 0, 1, -1), halo(q0, 0, 19, 1, 1, -1), halo(q0, 0, 14, 2, 1, -1), halo(q0, 0, 5, 3, 1, -1))
    mom_low = (halo(m3, 0, 3, 5, 3, 1, *shallow), halo(m2, 0, 3, 6, 1, 1, *shallow))
    mom_high = (halo(m3, 0, 3, 0, 3, -1), halo(m2, 0, 3, 1, 1, -1))
    relay_low = make(relay.at[1], got_relay.at[0], 1, 0, *shallow)
    relay_high = make(relay.at[0], got_relay.at[1], -1, 0)
    relay_deep = make(got.at[1], got.at[0], 1, 0, *deep)
    edge_low = make(edges.at[1], got_edges.at[0], 1, 0, *shallow)
    edge_high = make(edges.at[0], got_edges.at[1], -1, 0)

    start(*strips)
    start_far(posts_low, posts_high)
    start_near(posts_low, posts_high)
    start(*deeper)

    def forward(src, dst, mom, row):
        f = {
            q: shift_row(row_at(src, POST[q], row - LINKS[q][0]), LINKS[q][1], LINKS[q][2])
            for q in range(Q)
        }
        *u, rho = moments(f, row_at(p0, DRAG, row))
        for item, value in enumerate((*u, rho)):
            set_row(mom, item, row, value)
        if dst is not None:
            post = relax(f, rho, u, row_at(p0, SOLID, row))
            for q in range(Q):
                set_row(dst, POST[q], row, post[q])

    def backward(src, dst, mom, row):
        inc = {
            q: shift_row(row_at(src, ADJ[q], row + LINKS[q][0]), -LINKS[q][1], LINKS[q][2])
            for q in range(Q)
        }
        *u, rho = [row_at(mom, item, row) for item in range(4)]
        return pull(inc, rho, u, row_at(p0, DRAG, row), row_at(p0, SOLID, row))

    def middle(src, dst, mom, row):
        out, back = backward(src, dst, mom, row)
        for q in range(Q):
            set_row(dst, ADJ[q], row, out[q])
        place = pl.ds(pl.multiple_of((row + 8) * 8, 8), 8)
        sums[place, :] = back if mom is m3 else sums[place, :] + back

    def line(body, low, high, *refs):
        def one(k, _):
            body(*refs, jnp.where(paired_up, 7 - low - k, low + k))
            return 0

        lax.fori_loop(0, high - low, one, 0, unroll=min(4, high - low))

    def final(row):
        out, back = backward(q3, None, m0, row)
        there = pl.ds(row, 8, stride=8)
        for q in range(Q):
            out_ref[q, there, :] = out[q]
        grad_ref[there, :] = sums[pl.ds(pl.multiple_of((row + 8) * 8, 8), 8), :] + back

    line(forward, 1, 7, p0, p1, m1)
    line(forward, 2, 6, p1, p2, m2)
    line(forward, 3, 5, p2, None, m3)

    start_near(adj_low, adj_high)
    pl.when(along_x)(lambda: start_far(adj_low[:1], adj_high[:1]))

    received(*strips)
    first_half = lax.broadcasted_iota(jnp.int32, (8, 128), 0) < 4
    for place in range(PACK):
        low, high = got[1, 0, place], got[1, 1, place]
        relay[1, place] = jnp.where(first_half, pltpu.roll(low, 4, 0), high)
        relay[0, place] = jnp.where(first_half, low, pltpu.roll(high, 4, 0))
    start(relay_low, relay_high, relay_deep)
    pl.when(along_x)(lambda: start_far(adj_low[1:], adj_high[1:]))

    received_near(posts_low, posts_high)
    line(forward, -2, 1, p0, p1, m1)
    line(forward, -1, 2, p1, p2, m2)
    line(forward, 0, 3, p2, None, m3)
    start_near(mom_low, mom_high)
    left, right = mask_lanes(0, COLS, 64), mask_lanes(44, 44 + COLS, 64)
    near, far = jnp.where(paired_up, 2, 0), jnp.where(paired_up, 0, 2)

    def fill_strips(src, dst, first_item, count, tile):
        for item in range(count):
            slot, place = (first_item + item) % SLOTS, (first_item + item) // SLOTS
            by = slot * COLS
            here = pl.ds(pl.multiple_of(8 * tile, 8), 8)
            strip = dst[item, 8:16, :] if isinstance(tile, int) else own_strip(src, item, tile)
            low = pltpu.roll(got[tile, 0, place], (-by) % 128, 1)
            high = pltpu.roll(got[tile, 1, place], (44 - by) % 128, 1)
            dst[item, here, :] = jnp.where(left, low, jnp.where(right, high, strip))

    def take_low():
        received(relay_low)
        for place in range(PACK):
            both_sides = got_relay[0, place]
            got[0, 0, place], got[0, 1, place] = pltpu.roll(both_sides, 4, 0), both_sides

    def take_high():
        received(relay_high)
        for place in range(PACK):
            both_sides = got_relay[1, place]
            got[2, 0, place], got[2, 1, place] = both_sides, pltpu.roll(both_sides, 4, 0)

    def strip_forward(src, dst, mom):
        f = {q: shift_strip(src[POST[q]], *LINKS[q]) for q in range(Q)}
        *u, rho = moments(f, s0[DRAG])
        for item, value in enumerate((*u, rho)):
            mom[item] = value
        if dst is not None:
            post = relax(f, rho, u, s0[SOLID])
            for q in range(Q):
                dst[POST[q]] = post[q]

    for item in range(4):
        k0[item, 8:16, :] = own_strip(m0, item, 1)

    def strips_forward():
        strip_forward(s0, s1, k1)
        strip_forward(s1, s2, k2)
        strip_forward(s2, None, k3)

    def put_edges(side, wide, thin):
        for item in range(3):
            edges[side, 3 * item : 3 * item + 3, :] = k3[item, wide, :]
            edges[side, 9 + item : 10 + item, :] = k2[item, thin, :]

    def put_high():
        put_edges(1, slice(13, 16), slice(14, 15))
        start(edge_low)

    def put_low():
        put_edges(0, slice(8, 11), slice(9, 10))
        start(edge_high)

    def strip_backward(src, mom):
        inc = {q: shift_strip(src[ADJ[q]], *[-c for c in LINKS[q]]) for q in range(Q)}
        *u, rho = [mom[item] for item in range(4)]
        return pull(inc, rho, u, s0[DRAG], s0[SOLID])

    def strip_middle(src, dst, mom):
        out, back = strip_backward(src, mom)
        for q in range(Q):
            dst[ADJ[q]] = out[q]
        back_strip[...] = back if mom is k3 else back_strip[...] + back

    fill_strips(p0, s0, 0, ITEMS, 1)
    fill_strips(q0, t0, ITEMS, Q, 1)

    received_far(posts_low, posts_high)
    pl.when(along_z)(lambda: start_far(adj_low, adj_high))
    line(forward, 7, 10, p0, p1, m1)
    line(forward, 6, 9, p1, p2, m2)
    line(forward, 5, 8, p2, None, m3)
    start_far(mom_low, mom_high)

    pl.when(paired_up)(take_high)
    pl.when(paired_down)(take_low)
    fill_strips(p0, s0, 0, ITEMS, near)
    pl.when(paired_down)(take_high)

    @pl.when(jnp.logical_and(paired_up, shallow[1]))
    def _():
        take_low()

    pl.when(shallow[1])(lambda: fill_strips(p0, s0, 0, ITEMS, far))
    strips_forward()
    put_high()
    pl.when(shallow[1])(put_low)

    pl.when(last_x)(lambda: start_far(adj_low, adj_high))
    received_near(adj_low, adj_high)
    received_near(mom_low, mom_high)
    line(middle, -3, 5, q0, q1, m3)
    line(middle, -2, 4, q1, q2, m2)
    line(middle, -1, 3, q2, q3, m1)
    line(final, 0, 2)
    fill_strips(q0, t0, ITEMS, Q, near)

    line(middle, 5, 7, q0, q1, m3)
    line(middle, 4, 6, q1, q2, m2)
    line(middle, 3, 5, q2, q3, m1)
    line(final, 2, 4)

    received(*deeper, relay_deep)

    @pl.when(first_x)
    def _():
        def at(lowest, *refs):
            lax.fori_loop(0, 3, lambda k, _: (forward(*refs, k + lowest), 0)[1], 0, unroll=3)

        at(-5, p0, p1, m1)
        at(-4, p1, p2, m2)
        at(-3, p2, None, m3)
        fill_strips(p0, s0, 0, ITEMS, far)
        strips_forward()
        put_low()

    received_far(adj_low, adj_high)
    fill_strips(q0, t0, ITEMS, Q, far)

    received_far(mom_low, mom_high)
    received(edge_low, edge_high)

    def take_edges(side, wide, thin):
        for item in range(3):
            k3[item, wide, :] = got_edges[side, 3 * item : 3 * item + 3, :]
            k2[item, thin, :] = got_edges[side, 9 + item : 10 + item, :]

    pl.when(shallow[1])(lambda: take_edges(0, slice(5, 8), slice(6, 7)))
    take_edges(1, slice(16, 19), slice(17, 18))
    line(middle, 7, 11, q0, q1, m3)
    strip_middle(t0, t1, k3)
    line(middle, 6, 10, q1, q2, m2)
    strip_middle(t1, t2, k2)
    line(middle, 5, 9, q2, q3, m1)
    strip_middle(t2, t3, k1)
    strip_out, strip_back = strip_backward(t3, k0)
    for q in range(Q):
        t1[ADJ[q], 8:16, :] = strip_out[q][8:16]
    back_strip[8:16, :] = back_strip[8:16, :] + strip_back[8:16]
    line(final, 4, 8)

    first_cols, last_cols = mask_lanes(0, COLS, 128), mask_lanes(128 - COLS, 128, 128)

    def merge(ref, strip):
        for k, lane, chosen in ((0, 6, first_cols), (4, 70, first_cols), (3, 38 - 122, last_cols), (7, 102 - 122, last_cols)):
            here = slice(8 * k, 8 * k + 8)
            ref[here, :] = jnp.where(chosen, pltpu.roll(strip, (-lane) % 128, 1), ref[here, :])

    for q in range(Q):
        merge(out_ref.at[q], t1[ADJ[q], 8:16, :])
    merge(grad_ref, back_strip[8:16, :])

    for copy, sent_if, _ in copies:
        only_if(sent_if, copy.wait_send)


def to_tiles(a):
    lead = a.shape[:-3]
    n = len(lead)
    a = a.reshape(*lead, 2, 8, 4, 128)
    a = a.transpose(*range(n), n, n + 2, n + 1, n + 3)
    return a.reshape(*lead, 64, 128)


def from_tiles(a):
    lead = a.shape[:-2]
    n = len(lead)
    a = a.reshape(*lead, 2, 4, 8, 128)
    a = a.transpose(*range(n), n, n + 2, n + 1, n + 3)
    return a.reshape(*lead, 2, 8, 512)


def solution(mesh):
    n_gx, n_gy = mesh.shape["gx"], mesh.shape["gy"]

    def local(start, final_adjoint, resist, mask):
        any_space = pl.BlockSpec(memory_space=pl.ANY)
        vmem = pl.BlockSpec(memory_space=pltpu.VMEM)
        buf = lambda *shape: pltpu.VMEM(shape, F32)
        out, grad = pl.pallas_call(
            functools.partial(kernel, n_gx, n_gy),
            out_shape=(
                pltpu.VMEM((Q, 64, 128), F32),
                pltpu.VMEM((64, 128), F32),
            ),
            in_specs=[any_space] * 4,
            out_specs=[vmem, vmem],
            scratch_shapes=[
                buf(Q, 64, 128), buf(Q, 64, 128), buf(64, 128), pltpu.VMEM((64, 128), jnp.int32),
                buf(ITEMS, 192, 128), buf(ITEMS, 192, 128), buf(ITEMS, 192, 128),
                buf(Q, 192, 128), buf(Q, 192, 128), buf(Q, 192, 128), buf(Q, 192, 128),
                buf(4, 192, 128), buf(4, 192, 128), buf(4, 192, 128), buf(4, 192, 128), buf(192, 128),
                buf(ITEMS, 24, 128), buf(ITEMS, 24, 128), buf(ITEMS, 24, 128),
                buf(Q, 24, 128), buf(Q, 24, 128), buf(Q, 24, 128), buf(Q, 24, 128),
                buf(4, 24, 128), buf(4, 24, 128), buf(4, 24, 128), buf(4, 24, 128), buf(24, 128),
                buf(2, PACK, 8, 128), buf(3, 2, PACK, 8, 128), buf(2, 16, 128), buf(2, 16, 128),
                buf(2, PACK, 8, 128), buf(2, PACK, 8, 128),
                pltpu.SemaphoreType.DMA((4,)),
                pltpu.SemaphoreType.DMA((38,)),
                pltpu.SemaphoreType.DMA((38,)),
            ],
            compiler_params=pltpu.CompilerParams(
                collective_id=0, has_side_effects=True, vmem_limit_bytes=48 * 2**20
            ),
        )(*[pltpu.with_memory_space_constraint(to_tiles(a), pltpu.HBM) for a in (start, final_adjoint, resist, mask)])
        return from_tiles(out), from_tiles(grad)

    return jax.shard_map(
        local,
        mesh=mesh,
        in_specs=(
            P(None, None, "gx", "gy"),
            P(None, None, "gx", "gy"),
            P(None, "gx", "gy"),
            P(None, "gx", "gy"),
        ),
        out_specs=(P(None, None, "gx", "gy"), P(None, "gx", "gy")),
        check_vma=False,
    )
```
